512 devices in a mesh: dp: 64 (over y, z_hi, core), narrow: 8 (over x, z_lo).
Axes of the slice: x: 4, y: 8, z: 8 (z_hi: 4, z_lo: 2; z = z_hi * 2 + z_lo), core: 2. Of those that a mesh axis runs over, the one named last changes fastest.
Arguments:
- image_emb: bfloat16 [16384, 1152], P('dp'), may hold values from -0.1796875 to 0.1796875
- text_emb: bfloat16 [16384, 1152], P(('dp', 'narrow')), may hold values from -0.1796875 to 0.1796875
- positive: int32 [16384], P(('dp', 'narrow')), may hold values from 0 to 16383, as said below
- log_scale: float32 [1], replicated, may hold values from 2.3 to 3.4
- bias: float32 [1], replicated, may hold values from -4 to -2
Outputs:
- grad_image: bfloat16 [16384, 1152], P('dp')
- grad_text: bfloat16 [16384, 1152], P(('dp', 'narrow'))
The draws below stay inside these ranges and needn't reach their ends.
Inputs may be any that keep to these rules, and one draw needn't show every extreme that they name: `positive`: each image is paired with exactly one text: the b-th block of 256 texts names every image of the b-th block of 256 images once.
All inputs are finite; a program needn't handle non-finite values.
Results may differ from the reference program's by a relative error of at most 0.0066.
Values may be sent and summed in bfloat16 or wider, within the bound.
No kernel may reach another device: no remote copies, remote signals or barrier semaphores. Data moves between devices by JAX's collectives and lax.ppermute only.
A program may use at most 64 MiB of HBM per device.

```python
import jax
import jax.numpy as jnp
from jax import lax

D = 1152
TXT_DEV = 32
IMG_DP = 256
IMAGES = 16384
TEXTS = 16384
N_DP = 64
N_NARROW = 8


def draw_positive(key, part):
    key = jax.random.fold_in(key, 11)

    def one_block(block_key):
        return jax.random.permutation(block_key, IMG_DP).astype(jnp.int32)
    picked = jax.vmap(one_block)(jax.random.split(key, N_DP))
    offsets = (jnp.arange(N_DP, dtype=jnp.int32) * IMG_DP)[:, None]
    return (picked + offsets).reshape(-1).astype(jnp.int32)


def steps_of(own_key, dims, shards, smallest, high):
    loudness = 1.0
    for position, blocks in shards:
        heights = jax.random.uniform(jax.random.fold_in(jax.random.fold_in(own_key, 6), position), (blocks,), jnp.float32, smallest / len(shards), high / len(shards))
        loudness = loudness * jnp.repeat(jnp.exp(heights), dims[position] // blocks).reshape((-1,) + (1,) * (len(dims) - 1 - position))
    return loudness


def noise(rng, shape, scale, reach, cuts=(), kind=jnp.bfloat16):
    drawn = scale * jax.random.normal(rng, shape, jnp.float32)
    if cuts:
        drawn = drawn * steps_of(rng, shape, cuts, -0.22, 0.18)
    return jnp.clip(drawn, -reach, reach).astype(kind)


def setup_inputs(seed: int = 0) -> dict:
    key_of = jax.random.split(jax.random.key(seed), 6)
    return {
        "image_emb": noise(key_of[0], (IMAGES, D), 0.03, 0.1796875, ((0, 64),)),
        "text_emb": noise(key_of[1], (TEXTS, D), 0.03, 0.1796875, ((0, 512),)),
        "positive": draw_positive(jax.random.fold_in(key_of[5], 71), 0),
        "log_scale": jnp.clip(jax.random.uniform(key_of[3], (1,), jnp.float32, 2.3, 3.4), 2.3, 3.4),
        "bias": jnp.clip(jax.random.uniform(key_of[4], (1,), jnp.float32, -4.0, -2.0), -4.0, -2.0),
    }


epsilon = 1e-06

def unit_rows(values):
    as_float = values.astype(jnp.float32)
    row_norm = jnp.sqrt(lax.optimization_barrier(jnp.sum(as_float * as_float, axis=1, keepdims=True)) + epsilon)
    return (as_float / row_norm, row_norm)

def reference(image_emb, text_emb, positive, log_scale, bias):
    logit_scale = jnp.exp(log_scale[0])
    offset = bias[0]
    image_unit, image_norm = unit_rows(image_emb)
    text_unit, text_norm = unit_rows(text_emb)
    image_bf = image_unit.astype(jnp.bfloat16)
    text_bf = text_unit.astype(jnp.bfloat16)
    block_rows = TXT_DEV * N_NARROW
    block_count = TEXTS // block_rows
    image_rows = jnp.arange(IMAGES, dtype=jnp.int32)
    text_blocks = text_bf.reshape(block_count, block_rows, D)
    pos_blocks = positive.reshape(block_count, block_rows)

    def step_block(image_acc, block_item):
        block_text, block_pos = block_item
        cosine = jnp.dot(image_bf, block_text.T, preferred_element_type=jnp.float32)
        logits = logit_scale * cosine + offset
        hit = (image_rows[:, None] == block_pos[None, :]).astype(jnp.float32)
        pair_grad = jax.nn.sigmoid(logits) - hit
        grad_bf = pair_grad.astype(jnp.bfloat16)
        image_acc = image_acc + jnp.dot(grad_bf, block_text, preferred_element_type=jnp.float32)
        text_grads = jnp.dot(grad_bf.T, image_bf, preferred_element_type=jnp.float32)
        return (image_acc, text_grads)
    image_acc, text_grads = lax.scan(step_block, jnp.zeros((IMAGES, D), jnp.float32), (text_blocks, pos_blocks))
    grad_unit_image = logit_scale * image_acc
    grad_unit_text = logit_scale * text_grads.reshape(TEXTS, D)
    grad_image = (grad_unit_image - image_unit * lax.optimization_barrier(jnp.sum(image_unit * grad_unit_image, axis=1, keepdims=True))) / image_norm
    grad_text = (grad_unit_text - text_unit * lax.optimization_barrier(jnp.sum(text_unit * grad_unit_text, axis=1, keepdims=True))) / text_norm
    return (grad_image.astype(jnp.bfloat16), grad_text.astype(jnp.bfloat16))
```

```python
import jax
import jax.numpy as jnp
from jax import lax
from jax.sharding import Mesh, PartitionSpec as P

epsilon = 1e-06
AXES = ("y", "w", "c", "x", "l")
TEXT_AXES = ("y", "w")
IMAGE_AXES = ("c", "x", "l")
NARROW = ("x", "l")


def unit_rows(values):
    as_float = values.astype(jnp.float32)
    row_norm = jnp.sqrt(jnp.sum(as_float * as_float, axis=1, keepdims=True) + epsilon)
    return as_float / row_norm, row_norm


def spread(block, axes):
    count = lax.axis_size(axes)
    copies = jnp.broadcast_to(block[None], (count,) + block.shape)
    return lax.all_to_all(copies, axes, 0, 0, tiled=True)


def collect(terms, axes):
    count = lax.axis_size(axes)
    sent = terms.astype(jnp.bfloat16).reshape((count, -1, terms.shape[-1]))
    return jnp.sum(lax.all_to_all(sent, axes, 0, 0, tiled=True).astype(jnp.float32), axis=0)


def finish(grad_unit, unit, norm):
    along = jnp.sum(unit * grad_unit, axis=1, keepdims=True)
    return ((grad_unit - unit * along) / norm).astype(jnp.bfloat16)


def local(image_emb, text_emb, positive, log_scale, bias):
    scale = jnp.exp(log_scale[0])
    rows, width = image_emb.shape
    image_unit, image_norm = unit_rows(image_emb)
    text_unit, text_norm = unit_rows(text_emb)
    image_bf = image_unit.astype(jnp.bfloat16)
    text_bf = text_unit.astype(jnp.bfloat16)

    images = spread(image_bf, "c").reshape(-1, width)
    texts = spread(text_bf, TEXT_AXES).reshape(-1, width)
    slot = lax.axis_index(TEXT_AXES) * positive.shape[0]
    hits = lax.dynamic_update_slice_in_dim(jnp.full((texts.shape[0],), -1, jnp.int32), positive, slot, 0)

    first = lax.axis_index(TEXT_AXES) * images.shape[0]
    image_index = first + jnp.arange(images.shape[0], dtype=jnp.int32)
    cosine = lax.dot_general(images, texts, (((1,), (1,)), ((), ())), preferred_element_type=jnp.float32)
    hit = (image_index[:, None] == hits[None, :]).astype(jnp.float32)
    grad_bf = (jax.nn.sigmoid(scale * cosine + bias[0]) - hit).astype(jnp.bfloat16)
    text_terms = lax.dot_general(grad_bf, images, (((0,), (0,)), ((), ())), preferred_element_type=jnp.float32)
    image_terms = jnp.dot(grad_bf, texts, preferred_element_type=jnp.float32)

    own = lax.axis_index(NARROW) * (rows // 8)
    image_sum = scale * collect(image_terms, IMAGE_AXES)
    part = lax.dynamic_slice_in_dim(image_unit, own, rows // 8, 0)
    part_norm = lax.dynamic_slice_in_dim(image_norm, own, rows // 8, 0)
    grad_image = spread(finish(image_sum, part, part_norm), NARROW).reshape(rows, width)

    grad_text = finish(scale * collect(text_terms, TEXT_AXES), text_unit, text_norm)
    return grad_image, grad_text


def solution(mesh):
    fine = Mesh(mesh.devices.reshape(8, 4, 2, 4, 2), AXES)
    dp, every = ("y", "w", "c"), AXES
    in_specs = (P(dp, None), P(every, None), P(every), P(), P())
    out_specs = (P(dp, None), P(every, None))
    return jax.shard_map(local, mesh=fine, in_specs=in_specs, out_specs=out_specs, check_vma=False)
```

```python
import jax
import jax.numpy as jnp
from jax import lax
from jax.sharding import Mesh, PartitionSpec as P

epsilon = 1e-06
AXES = ("yh", "yl", "w", "c", "x", "l")
Y, Z = ("yh", "yl"), ("w", "l")
NARROW = ("x", "l")
GROUP = ("yl", "x", "l")
BF16, F32 = jnp.bfloat16, jnp.float32


def unit_rows(values):
    as_float = values.astype(F32)
    row_norm = jnp.sqrt(jnp.sum(as_float * as_float, axis=1, keepdims=True) + epsilon)
    return as_float / row_norm, row_norm


def swap(block, axis):
    return lax.ppermute(block, axis, [(0, 1), (1, 0)])


def route(axes, distance):
    count = lax.axis_size(axes)
    pairs = []
    for i in range(count):
        sign = 1 if (i + distance) % 2 == 0 else -1
        pairs.append((i, (i + sign * distance) % count))
    return pairs


def fan_out(block, axes, distance):
    return lax.ppermute(block, axes, route(axes, distance))


def fan_in(terms, axes, distance):
    back = [(target, source) for source, target in route(axes, distance)]
    return lax.ppermute(terms.astype(BF16), axes, back).astype(F32)


def finish(grad_unit, unit, norm):
    along = jnp.sum(unit * grad_unit, axis=1, keepdims=True)
    return ((grad_unit - unit * along) / norm).astype(BF16)


def local(image_emb, text_emb, positive, log_scale, bias):
    scale = jnp.exp(log_scale[0])
    rows, width = image_emb.shape
    mine = text_emb.shape[0]
    text_unit, text_norm = unit_rows(text_emb)
    text_bf = text_unit.astype(BF16)
    along_y = jnp.concatenate([text_bf] + [fan_out(text_bf, Y, d) for d in (1, 2, 3)], axis=0)

    image_unit, image_norm = unit_rows(image_emb)
    image_bf = image_unit.astype(BF16)
    beyond = swap(image_bf, "yl")
    images = jnp.concatenate([image_bf, swap(image_bf, "c"), beyond, swap(beyond, "c")], axis=0)

    wanted = positive - lax.axis_index(("yh", "yl", "w", "c")) * rows
    hit = jnp.arange(rows, dtype=jnp.int32)[:, None] == wanted[None, :]

    grads, texts, returned = [], [], []
    for d in (0, 1, 2, 3):
        block = along_y if d == 0 else fan_out(along_y, Z, d)
        cosine = lax.dot_general(images, block, (((1,), (1,)), ((), ())), preferred_element_type=F32)
        grad = jax.nn.sigmoid(scale * cosine + bias[0])
        if d == 0:
            padded = jnp.pad(hit.astype(F32), ((0, grad.shape[0] - rows), (0, grad.shape[1] - mine)))
            grad = grad - padded
        grad = grad.astype(BF16)
        terms = lax.dot_general(grad, images, (((0,), (0,)), ((), ())), preferred_element_type=F32)
        returned.append(terms if d == 0 else fan_in(terms, Z, d))
        grads.append(grad)
        texts.append(block)

    image_terms = jnp.dot(jnp.concatenate(grads, axis=1), jnp.concatenate(texts, axis=0), preferred_element_type=F32)
    image_terms = image_terms.reshape(2, 2, rows, width)
    pairs = image_terms[:, 0] + swap(image_terms[:, 1].astype(BF16), "c").astype(F32)
    upper = lax.axis_index("yl") == 1
    pairs = jnp.where(upper, pairs[::-1], pairs).astype(BF16).reshape(16, rows // 8, width)
    image_sum = scale * jnp.sum(lax.all_to_all(pairs, GROUP, 0, 0, tiled=True).astype(F32), axis=0)
    own = lax.axis_index(NARROW) * (rows // 8)
    part = lax.dynamic_slice_in_dim(image_unit, own, rows // 8, 0)
    part_norm = lax.dynamic_slice_in_dim(image_norm, own, rows // 8, 0)
    done = finish(image_sum, part, part_norm)
    grad_image = lax.all_to_all(jnp.broadcast_to(done[None], (8,) + done.shape), NARROW, 0, 0, tiled=True)

    text_sum = sum(returned).reshape(4, mine, width)
    text_sum = text_sum[0] + sum(fan_in(text_sum[d], Y, d) for d in (1, 2, 3))
    grad_text = finish(scale * text_sum, text_unit, text_norm)
    return grad_image.reshape(rows, width), grad_text


def solution(mesh):
    fine = Mesh(mesh.devices.reshape(4, 2, 4, 2, 4, 2), AXES)
    dp = ("yh", "yl", "w", "c")
    in_specs = (P(dp, None), P(AXES, None), P(AXES), P(), P())
    out_specs = (P(dp, None), P(AXES, None))
    return jax.shard_map(local, mesh=fine, in_specs=in_specs, out_specs=out_specs, check_vma=False)
```

```python
import jax
import jax.numpy as jnp
from jax import lax
from jax.sharding import Mesh, PartitionSpec as P

epsilon = 1e-06
AXES = ("yh", "yl", "w", "c", "x", "l")
TEXT_GROUP = ("yh", "w")
NARROW = ("x", "l")
BF16, F32 = jnp.bfloat16, jnp.float32


def unit_rows(values):
    as_float = values.astype(F32)
    row_norm = jnp.sqrt(jnp.sum(as_float * as_float, axis=1, keepdims=True) + epsilon)
    return as_float / row_norm, row_norm


def swap(block, axis):
    return lax.ppermute(block, axis, [(0, 1), (1, 0)])


def spread(block, axes):
    count = lax.axis_size(axes)
    copies = jnp.broadcast_to(block[None], (count,) + block.shape)
    return lax.all_to_all(copies, axes, 0, 0, tiled=True).reshape((-1,) + block.shape[1:])


def collect(terms, axes):
    got = lax.all_to_all(terms.astype(BF16), axes, 0, 0, tiled=True)
    return jnp.sum(got.astype(F32), axis=0)


def finish(grad_unit, unit, norm):
    along = jnp.sum(unit * grad_unit, axis=1, keepdims=True)
    return ((grad_unit - unit * along) / norm).astype(BF16)


def local(image_emb, text_emb, positive, log_scale, bias):
    scale = jnp.exp(log_scale[0])
    rows, width = image_emb.shape
    mine = text_emb.shape[0]
    text_unit, text_norm = unit_rows(text_emb)
    texts = spread(text_unit.astype(BF16), TEXT_GROUP)

    image_unit, image_norm = unit_rows(image_emb)
    image_bf = image_unit.astype(BF16)
    beyond = swap(image_bf, "yl")
    images = jnp.concatenate([image_bf, swap(image_bf, "c"), beyond, swap(beyond, "c")], axis=0)

    wanted = positive - lax.axis_index(("yh", "yl", "w", "c")) * rows
    slot = lax.axis_index(TEXT_GROUP) * mine
    wanted = lax.dynamic_update_slice_in_dim(jnp.full((texts.shape[0],), -1, jnp.int32), wanted, slot, 0)
    hit = (jnp.arange(images.shape[0], dtype=jnp.int32)[:, None] == wanted[None, :]).astype(F32)

    cosine = lax.dot_general(images, texts, (((1,), (1,)), ((), ())), preferred_element_type=F32)
    grad = (jax.nn.sigmoid(scale * cosine + bias[0]) - hit).astype(BF16)
    image_terms = jnp.dot(grad, texts, preferred_element_type=F32).reshape(2, 2, rows, width)
    text_terms = lax.dot_general(grad, images, (((0,), (0,)), ((), ())), preferred_element_type=F32)

    pairs = image_terms[:, 0] + swap(image_terms[:, 1].astype(BF16), "c").astype(F32)
    pairs = pairs.reshape(2, 8, rows // 8, width).transpose(1, 0, 2, 3)
    part_terms = collect(pairs, NARROW)
    image_sum = scale * (part_terms[0] + swap(part_terms[1].astype(BF16), "yl").astype(F32))
    own = lax.axis_index(NARROW) * (rows // 8)
    part = lax.dynamic_slice_in_dim(image_unit, own, rows // 8, 0)
    part_norm = lax.dynamic_slice_in_dim(image_norm, own, rows // 8, 0)
    grad_image = spread(finish(image_sum, part, part_norm), NARROW)

    text_sum = collect(text_terms.reshape(16, mine, width), TEXT_GROUP)
    grad_text = finish(scale * text_sum, text_unit, text_norm)
    return grad_image, grad_text


def solution(mesh):
    fine = Mesh(mesh.devices.reshape(4, 2, 4, 2, 4, 2), AXES)
    dp = ("yh", "yl", "w", "c")
    in_specs = (P(dp, None), P(AXES, None), P(AXES), P(), P())
    out_specs = (P(dp, None), P(AXES, None))
    return jax.shard_map(local, mesh=fine, in_specs=in_specs, out_specs=out_specs, check_vma=False)
```

```python
import jax
import jax.numpy as jnp
from jax import lax
from jax.sharding import Mesh, PartitionSpec as P

epsilon = 1e-06
AXES = ("yh", "yl", "w", "c", "x", "l")
Z = ("w", "l")
DISTANCES = (3, 2, 1)
NARROW = ("x", "l")
BF16, F32 = jnp.bfloat16, jnp.float32


def unit_rows(values):
    as_float = values.astype(F32)
    row_norm = jnp.sqrt(jnp.sum(as_float * as_float, axis=1, keepdims=True) + epsilon)
    return as_float / row_norm, row_norm


def swap(block, axis):
    return lax.ppermute(block, axis, [(0, 1), (1, 0)])


def route(axes, distance):
    count = lax.axis_size(axes)
    pairs = []
    for i in range(count):
        sign = 1 if (i + distance) % 2 == 0 else -1
        pairs.append((i, (i + sign * distance) % count))
    return pairs


def fan_out(block, axes, distance):
    return lax.ppermute(block, axes, route(axes, distance))


def fan_in(terms, axes, distance):
    back = [(target, source) for source, target in route(axes, distance)]
    return lax.ppermute(terms, axes, back)


def spread(block, axes):
    count = lax.axis_size(axes)
    copies = jnp.broadcast_to(block[None], (count,) + block.shape)
    return lax.all_to_all(copies, axes, 0, 0, tiled=True).reshape((-1,) + block.shape[1:])


def collect(terms, axes):
    got = lax.all_to_all(terms.astype(BF16), axes, 0, 0, tiled=True)
    return jnp.sum(got.astype(F32), axis=0)


def finish(grad_unit, unit, norm):
    along = jnp.sum(unit * grad_unit, axis=1, keepdims=True)
    return ((grad_unit - unit * along) / norm).astype(BF16)


def local(image_emb, text_emb, positive, log_scale, bias):
    scale = jnp.exp(log_scale[0])
    rows, width = image_emb.shape
    mine = text_emb.shape[0]
    text_unit, text_norm = unit_rows(text_emb)
    along_y = spread(text_unit.astype(BF16), "yh")
    blocks = [along_y] + [fan_out(along_y, Z, d) for d in DISTANCES]

    image_unit, image_norm = unit_rows(image_emb)
    image_bf = image_unit.astype(BF16)
    beyond = swap(image_bf, "yl")
    images = jnp.concatenate([image_bf, swap(image_bf, "c"), beyond, swap(beyond, "c")], axis=0)

    wanted = positive - lax.axis_index(("yh", "yl", "w", "c")) * rows
    slot = lax.axis_index("yh") * mine
    wanted = lax.dynamic_update_slice_in_dim(jnp.full((along_y.shape[0],), -1, jnp.int32), wanted, slot, 0)
    hit = (jnp.arange(images.shape[0], dtype=jnp.int32)[:, None] == wanted[None, :]).astype(F32)

    grads, terms = [], []
    for k, block in enumerate(blocks):
        cosine = lax.dot_general(images, block, (((1,), (1,)), ((), ())), preferred_element_type=F32)
        grad = jax.nn.sigmoid(scale * cosine + bias[0])
        grad = (grad - hit if k == 0 else grad).astype(BF16)
        term = lax.dot_general(grad, images, (((0,), (0,)), ((), ())), preferred_element_type=F32)
        terms.append(term if k == 0 else fan_in(term.astype(BF16), Z, DISTANCES[k - 1]))
        grads.append(grad)
    image_terms = jnp.dot(jnp.concatenate(grads, axis=1), jnp.concatenate(blocks, axis=0), preferred_element_type=F32)
    image_terms = image_terms.reshape(2, 2, rows, width)

    pairs = image_terms[:, 0] + swap(image_terms[:, 1].astype(BF16), "c").astype(F32)
    pairs = pairs.reshape(2, 8, rows // 8, width).transpose(1, 0, 2, 3)
    part_terms = collect(pairs, NARROW)
    part_terms, terms = lax.optimization_barrier((part_terms, terms))
    image_sum = scale * (part_terms[0] + swap(part_terms[1].astype(BF16), "yl").astype(F32))
    own = lax.axis_index(NARROW) * (rows // 8)
    part = lax.dynamic_slice_in_dim(image_unit, own, rows // 8, 0)
    part_norm = lax.dynamic_slice_in_dim(image_norm, own, rows // 8, 0)
    grad_image = spread(finish(image_sum, part, part_norm), NARROW)

    text_sum = sum(term.astype(F32) for term in terms)
    text_sum = collect(text_sum.reshape(4, mine, width), "yh")
    grad_text = finish(scale * text_sum, text_unit, text_norm)
    return grad_image, grad_text


def solution(mesh):
    fine = Mesh(mesh.devices.reshape(4, 2, 4, 2, 4, 2), AXES)
    dp = ("yh", "yl", "w", "c")
    in_specs = (P(dp, None), P(AXES, None), P(AXES), P(), P())
    out_specs = (P(dp, None), P(AXES, None))
    return jax.shard_map(local, mesh=fine, in_specs=in_specs, out_specs=out_specs, check_vma=False)
```

```python
import jax
import jax.numpy as jnp
from jax import lax
from jax.sharding import Mesh, PartitionSpec as P

epsilon = 1e-06
AXES = ("yh", "yl", "w", "c", "x", "l")
TEXT_GROUP = ("yh", "w")
NARROW = ("x", "l")
BF16, F32 = jnp.bfloat16, jnp.float32


def unit_rows(values):
    as_float = values.astype(F32)
    row_norm = jnp.sqrt(jnp.sum(as_float * as_float, axis=1, keepdims=True) + epsilon)
    return as_float / row_norm, row_norm


def swap(block, axis):
    return lax.ppermute(block, axis, [(0, 1), (1, 0)])


def shift(block, axis, distance):
    count = lax.axis_size(axis)
    return lax.ppermute(block, axis, [(i, (i + distance) % count) for i in range(count)])


def spread(block, axes):
    count = lax.axis_size(axes)
    copies = jnp.broadcast_to(block[None], (count,) + block.shape)
    return lax.all_to_all(copies, axes, 0, 0, tiled=True).reshape((-1,) + block.shape[1:])


def collect(terms, axes):
    got = lax.all_to_all(terms.astype(BF16), axes, 0, 0, tiled=True)
    return jnp.sum(got.astype(F32), axis=0)


def finish(grad_unit, unit, norm):
    along = jnp.sum(unit * grad_unit, axis=1, keepdims=True)
    return ((grad_unit - unit * along) / norm).astype(BF16)


def local(image_emb, text_emb, positive, log_scale, bias):
    scale = jnp.exp(log_scale[0])
    rows, width = image_emb.shape
    mine = text_emb.shape[0]
    n_x = lax.axis_size("x")
    x = lax.axis_index("x")
    quarter = rows // n_x

    part = swap(lax.dynamic_slice_in_dim(image_emb, x * quarter, quarter, 0), "yl")
    beyond = [part] + [shift(part, "x", d) for d in range(1, n_x)]
    chip = jnp.concatenate([image_emb] + beyond, axis=0)
    images = jnp.concatenate([chip, swap(chip, "c")], axis=0)
    image_bf = unit_rows(images)[0].astype(BF16)

    texts = spread(text_emb, TEXT_GROUP)
    text_bf = unit_rows(texts)[0].astype(BF16)

    wanted = positive - lax.axis_index(("yh", "yl", "w", "c")) * rows
    slot = lax.axis_index(TEXT_GROUP) * mine
    wanted = lax.dynamic_update_slice_in_dim(jnp.full((texts.shape[0],), -1, jnp.int32), wanted, slot, 0)
    hit = (jnp.arange(images.shape[0], dtype=jnp.int32)[:, None] == wanted[None, :]).astype(F32)

    cosine = lax.dot_general(image_bf, text_bf, (((1,), (1,)), ((), ())), preferred_element_type=F32)
    grad = (jax.nn.sigmoid(scale * cosine + bias[0]) - hit).astype(BF16)
    text_terms = lax.dot_general(grad, image_bf, (((0,), (0,)), ((), ())), preferred_element_type=F32).astype(BF16)
    text_terms, grad = lax.optimization_barrier((text_terms, grad))
    text_sum = collect(text_terms.reshape(-1, mine, width), TEXT_GROUP)

    image_terms = jnp.dot(grad, text_bf, preferred_element_type=F32).reshape(2, 2 * rows, width)
    both = image_terms[0] + swap(image_terms[1].astype(BF16), "c").astype(F32)
    own, other = both[:rows], both[rows:].reshape(n_x, quarter, width)
    own_sum, other_sum = lax.dynamic_slice_in_dim(own, x * quarter, quarter, 0), other[0]
    for d in range(1, n_x):
        sent = lax.dynamic_slice_in_dim(own, lax.rem(x + d, n_x) * quarter, quarter, 0)
        got = shift(jnp.concatenate([sent, other[n_x - d]], axis=0).astype(BF16), "x", d).astype(F32)
        own_sum, other_sum = own_sum + got[:quarter], other_sum + got[quarter:]
    lower = lax.axis_index("yl") == 0
    pair = jnp.stack([jnp.where(lower, own_sum, other_sum), jnp.where(lower, other_sum, own_sum)])
    image_sum = scale * collect(pair.reshape(4, rows // 8, width), ("yl", "l"))

    first = lax.axis_index(NARROW) * (rows // 8)
    part_unit, part_norm = unit_rows(lax.dynamic_slice_in_dim(image_emb, first, rows // 8, 0))
    grad_image = spread(finish(image_sum, part_unit, part_norm), NARROW)

    text_unit, text_norm = unit_rows(text_emb)
    grad_text = finish(scale * text_sum, text_unit, text_norm)
    return grad_image, grad_text


def solution(mesh):
    fine = Mesh(mesh.devices.reshape(4, 2, 4, 2, 4, 2), AXES)
    dp = ("yh", "yl", "w", "c")
    in_specs = (P(dp, None), P(AXES, None), P(AXES), P(), P())
    out_specs = (P(dp, None), P(AXES, None))
    return jax.shard_map(local, mesh=fine, in_specs=in_specs, out_specs=out_specs, check_vma=False)
```

```python
import jax
import jax.numpy as jnp
from jax import lax
from jax.sharding import Mesh, PartitionSpec as P

epsilon = 1e-06
AXES = ("yh", "yl", "w", "c", "x", "l")
TEXT_GROUP = ("yh", "w")
NARROW = ("x", "l")
BF16, F32 = jnp.bfloat16, jnp.float32


def unit_rows(values):
    as_float = values.astype(F32)
    row_norm = jnp.sqrt(jnp.sum(as_float * as_float, axis=1, keepdims=True) + epsilon)
    return as_float / row_norm, row_norm


def swap(block, axis):
    return lax.ppermute(block, axis, [(0, 1), (1, 0)])


def shift(block, axis, distance):
    count = lax.axis_size(axis)
    return lax.ppermute(block, axis, [(i, (i + distance) % count) for i in range(count)])


def spread(block, axes):
    count = lax.axis_size(axes)
    copies = jnp.broadcast_to(block[None], (count,) + block.shape)
    return lax.all_to_all(copies, axes, 0, 0, tiled=True).reshape((-1,) + block.shape[1:])


def collect(terms, axes):
    got = lax.all_to_all(terms.astype(BF16), axes, 0, 0, tiled=True)
    return jnp.sum(got.astype(F32), axis=0)


def finish(grad_unit, unit, norm):
    along = jnp.sum(unit * grad_unit, axis=1, keepdims=True)
    return ((grad_unit - unit * along) / norm).astype(BF16)


def local(image_emb, text_emb, positive, log_scale, bias):
    scale = jnp.exp(log_scale[0])
    rows, width = image_emb.shape
    mine = text_emb.shape[0]
    n_x = lax.axis_size("x")
    x = lax.axis_index("x")
    quarter = rows // n_x

    part = swap(lax.dynamic_slice_in_dim(image_emb, x * quarter, quarter, 0), "yl")
    beyond = [part] + [shift(part, "x", d) for d in range(1, n_x)]
    chip = jnp.concatenate([image_emb] + beyond, axis=0)
    images = jnp.concatenate([chip, swap(chip, "c")], axis=0)
    image_bf = unit_rows(images)[0].astype(BF16)

    texts = spread(text_emb, TEXT_GROUP)
    text_bf = unit_rows(texts)[0].astype(BF16)

    wanted = positive - lax.axis_index(("yh", "yl", "w", "c")) * rows
    slot = lax.axis_index(TEXT_GROUP) * mine
    wanted = lax.dynamic_update_slice_in_dim(jnp.full((texts.shape[0],), -1, jnp.int32), wanted, slot, 0)
    hit = (jnp.arange(images.shape[0], dtype=jnp.int32)[:, None] == wanted[None, :]).astype(F32)

    cosine = lax.dot_general(image_bf, text_bf, (((1,), (1,)), ((), ())), preferred_element_type=F32)
    grad = (jax.nn.sigmoid(scale * cosine + bias[0]) - hit).astype(BF16)
    text_terms = lax.dot_general(grad, image_bf, (((0,), (0,)), ((), ())), preferred_element_type=F32).astype(BF16)
    text_terms, grad = lax.optimization_barrier((text_terms, grad))
    text_sum = collect(text_terms.reshape(-1, mine, width), TEXT_GROUP)

    image_terms = jnp.dot(grad, text_bf, preferred_element_type=F32).reshape(2, 2 * rows, width)
    both = image_terms[0] + swap(image_terms[1].astype(BF16), "c").astype(F32)
    own, other = both[:rows], both[rows:].reshape(n_x, quarter, width)
    own_sum, other_sum = lax.dynamic_slice_in_dim(own, x * quarter, quarter, 0), other[0]
    for d in range(1, n_x):
        sent = lax.dynamic_slice_in_dim(own, lax.rem(x + d, n_x) * quarter, quarter, 0)
        got = shift(jnp.concatenate([sent, other[n_x - d]], axis=0).astype(BF16), "x", d).astype(F32)
        own_sum, other_sum = own_sum + got[:quarter], other_sum + got[quarter:]
    lower = lax.axis_index("yl") == 0
    pair = jnp.stack([jnp.where(lower, own_sum, other_sum), jnp.where(lower, other_sum, own_sum)])
    pair, text_sum = lax.optimization_barrier((pair, text_sum))
    image_sum = scale * collect(pair.reshape(4, rows // 8, width), ("yl", "l"))

    first = lax.axis_index(NARROW) * (rows // 8)
    part_unit, part_norm = unit_rows(lax.dynamic_slice_in_dim(image_emb, first, rows // 8, 0))
    grad_image = spread(finish(image_sum, part_unit, part_norm), NARROW)

    text_unit, text_norm = unit_rows(text_emb)
    grad_text = finish(scale * text_sum, text_unit, text_norm)
    return grad_image, grad_text


def solution(mesh):
    fine = Mesh(mesh.devices.reshape(4, 2, 4, 2, 4, 2), AXES)
    dp = ("yh", "yl", "w", "c")
    in_specs = (P(dp, None), P(AXES, None), P(AXES), P(), P())
    out_specs = (P(dp, None), P(AXES, None))
    return jax.shard_map(local, mesh=fine, in_specs=in_specs, out_specs=out_specs, check_vma=False)
```

```python
import jax
import jax.numpy as jnp
from jax import lax
from jax.experimental import pallas as pl
from jax.experimental.pallas import tpu as pltpu
from jax.sharding import Mesh, PartitionSpec as P

epsilon = 1e-06
AXES = ("yh", "yl", "w", "c", "x", "l")
CLASSES = ((0, 3, 5, 6), (1, 2, 4, 7))
RINGS = ("yh", "yl", "w", "l")
TEXT_GROUPS = [[y * 8 + z for y in of_y for z in of_z] for of_y in CLASSES for of_z in CLASSES]
NARROW = ("x", "l")
BF16, F32 = jnp.bfloat16, jnp.float32


def unit_rows(values):
    as_float = values.astype(F32)
    row_norm = jnp.sqrt(jnp.sum(as_float * as_float, axis=1, keepdims=True) + epsilon)
    return as_float / row_norm, row_norm


def swap(block, axis):
    return lax.ppermute(block, axis, [(0, 1), (1, 0)])


def shift(block, axis, distance):
    count = lax.axis_size(axis)
    return lax.ppermute(block, axis, [(i, (i + distance) % count) for i in range(count)])


def exchange(blocks, axes, groups=None):
    return lax.all_to_all(blocks, axes, 0, 0, axis_index_groups=groups, tiled=True)


def first_copies(x, image_emb, text_emb, quarter, peers):
    mine, width = text_emb.shape

    def body(x_ref, image_ref, text_ref, quarter_ref, copies_ref):
        start = pl.multiple_of(x_ref[0] * quarter, quarter)
        quarter_ref[...] = image_ref[pl.ds(start, quarter), :]
        for k in range(peers):
            copies_ref[k] = text_ref[...]

    whole = pl.BlockSpec(memory_space=pltpu.VMEM)
    return pl.pallas_call(
        body,
        out_shape=(
            jax.ShapeDtypeStruct((quarter, width), BF16),
            jax.ShapeDtypeStruct((peers, mine, width), BF16),
        ),
        in_specs=[pl.BlockSpec(memory_space=pltpu.SMEM), whole, whole],
        out_specs=(whole, whole),
        name="first_copies",
    )(x, image_emb, text_emb)


def finish(terms, rows, scale):
    count, height, width = terms.shape

    def body(scale_ref, terms_ref, rows_ref, out_ref):
        unit, norm = unit_rows(rows_ref[...])
        total = terms_ref[0].astype(F32)
        for k in range(1, count):
            total = total + terms_ref[k].astype(F32)
        total = scale_ref[0] * total
        along = jnp.sum(unit * total, axis=1, keepdims=True)
        out_ref[...] = ((total - unit * along) / norm).astype(BF16)

    whole = pl.BlockSpec(memory_space=pltpu.VMEM)
    return pl.pallas_call(
        body,
        out_shape=jax.ShapeDtypeStruct((height, width), BF16),
        in_specs=[pl.BlockSpec(memory_space=pltpu.SMEM), whole, whole],
        out_specs=whole,
        name="finish",
    )(scale.reshape(1), terms, rows)


def local(image_emb, text_emb, positive, log_scale, bias):
    scale = jnp.exp(log_scale[0])
    rows, width = image_emb.shape
    mine = text_emb.shape[0]
    peers = len(TEXT_GROUPS[0])
    n_x = lax.axis_size("x")
    x = lax.axis_index("x")
    upper = lax.axis_index("yl") == 1
    quarter = rows // n_x

    part, copies = first_copies(x.astype(jnp.int32).reshape(1), image_emb, text_emb, quarter, peers)
    part = swap(part, "yl")
    texts = exchange(copies, RINGS, TEXT_GROUPS).reshape(-1, width)
    around = [part] + [shift(part, "x", n_x - d) for d in range(1, n_x)]
    beyond = lax.dynamic_slice_in_dim(jnp.concatenate(around * 2, axis=0), lax.rem(n_x - x, n_x) * quarter, rows, 0)
    chip = jnp.concatenate([jnp.where(upper, beyond, image_emb), jnp.where(upper, image_emb, beyond)], axis=0)
    near = unit_rows(chip)[0].astype(BF16)
    far = swap(near, "c")
    text_bf = unit_rows(texts)[0].astype(BF16)

    wanted = positive - lax.axis_index(("yh", "yl", "w", "c")) * rows + lax.axis_index("yl") * rows
    slot = lax.axis_index(("yh", "w")) * mine
    wanted = lax.dynamic_update_slice_in_dim(jnp.full((texts.shape[0],), -1, jnp.int32), wanted, slot, 0)
    hit = (jnp.arange(near.shape[0], dtype=jnp.int32)[:, None] == wanted[None, :]).astype(F32)

    def pair_grad(images):
        cosine = lax.dot_general(images, text_bf, (((1,), (1,)), ((), ())), preferred_element_type=F32)
        return jax.nn.sigmoid(scale * cosine + bias[0])

    far_grad = pair_grad(far).astype(BF16)
    far_terms = swap(jnp.dot(far_grad, text_bf, preferred_element_type=F32).astype(BF16), "c")
    near_grad = (pair_grad(near) - hit).astype(BF16)
    near_terms = jnp.dot(near_grad, text_bf, preferred_element_type=F32) + far_terms.astype(F32)
    near_terms = near_terms.astype(BF16).reshape(peers, rows // 8, width)
    first = lax.axis_index(NARROW) * (rows // 8)
    image_rows = lax.dynamic_slice_in_dim(image_emb, first, rows // 8, 0)
    done = finish(exchange(near_terms, ("yl", "x", "l")), image_rows, scale)

    over_images = (((0,), (0,)), ((), ()))
    text_terms = lax.dot_general(near_grad, near, over_images, preferred_element_type=F32)
    text_terms = text_terms + lax.dot_general(far_grad, far, over_images, preferred_element_type=F32)
    text_terms, done = lax.optimization_barrier((text_terms.astype(BF16), done))
    grad_image = lax.all_gather(done, NARROW, axis=0, tiled=True)
    grad_text = finish(exchange(text_terms.reshape(peers, mine, width), RINGS, TEXT_GROUPS), text_emb, scale)
    return grad_image, grad_text


def solution(mesh):
    fine = Mesh(mesh.devices.reshape(4, 2, 4, 2, 4, 2), AXES)
    dp = ("yh", "yl", "w", "c")
    in_specs = (P(dp, None), P(AXES, None), P(AXES), P(), P())
    out_specs = (P(dp, None), P(AXES, None))
    return jax.shard_map(local, mesh=fine, in_specs=in_specs, out_specs=out_specs, check_vma=False)
```

```python
import jax
import jax.numpy as jnp
from jax import lax
from jax.experimental import pallas as pl
from jax.experimental.pallas import tpu as pltpu
from jax.sharding import Mesh, PartitionSpec as P

epsilon = 1e-06
AXES = ("yh", "yl", "wh", "wl", "c", "x", "l")
SIZES = (4, 2, 2, 2, 2, 4, 2)
Y_GROUPS = ((0, 3, 5, 6), (1, 2, 4, 7))
Z_GROUPS = ((0, 7), (1, 6), (2, 5), (3, 4))
RINGS = ("yh", "yl", "wh", "wl", "l")
TEXT_GROUPS = [[y * 8 + z for y in of_y for z in of_z] for of_y in Y_GROUPS for of_z in Z_GROUPS]
NARROW = ("x", "l")
BF16, F32 = jnp.bfloat16, jnp.float32


def unit_rows(values):
    as_float = values.astype(F32)
    row_norm = jnp.sqrt(jnp.sum(as_float * as_float, axis=1, keepdims=True) + epsilon)
    return as_float / row_norm, row_norm


def swap(block, axes):
    count = lax.axis_size(axes)
    return lax.ppermute(block, axes, [(i, count - 1 - i) for i in range(count)])


def shift(block, axis, distance):
    count = lax.axis_size(axis)
    return lax.ppermute(block, axis, [(i, (i + distance) % count) for i in range(count)])


def exchange(blocks, axes, groups=None):
    return lax.all_to_all(blocks, axes, 0, 0, axis_index_groups=groups, tiled=True)


def first_copies(x, image_emb, text_emb, quarter, peers):
    mine, width = text_emb.shape

    def body(x_ref, image_ref, text_ref, quarter_ref, copies_ref):
        start = pl.multiple_of(x_ref[0] * quarter, quarter)
        quarter_ref[...] = image_ref[pl.ds(start, quarter), :]
        for k in range(peers):
            copies_ref[k] = text_ref[...]

    whole = pl.BlockSpec(memory_space=pltpu.VMEM)
    return pl.pallas_call(
        body,
        out_shape=(
            jax.ShapeDtypeStruct((quarter, width), BF16),
            jax.ShapeDtypeStruct((peers, mine, width), BF16),
        ),
        in_specs=[pl.BlockSpec(memory_space=pltpu.SMEM), whole, whole],
        out_specs=(whole, whole),
        name="first_copies",
    )(x, image_emb, text_emb)


def finish(terms, rows, scale, peers):
    count, height, width = terms.shape

    def body(scale_ref, terms_ref, rows_ref, out_ref):
        unit, norm = unit_rows(rows_ref[...])
        total = terms_ref[0].astype(F32)
        for k in range(1, count):
            total = total + terms_ref[k].astype(F32)
        total = scale_ref[0] * total
        along = jnp.sum(unit * total, axis=1, keepdims=True)
        grad = ((total - unit * along) / norm).astype(BF16)
        for k in range(peers):
            out_ref[k] = grad

    whole = pl.BlockSpec(memory_space=pltpu.VMEM)
    return pl.pallas_call(
        body,
        out_shape=jax.ShapeDtypeStruct((peers, height, width), BF16),
        in_specs=[pl.BlockSpec(memory_space=pltpu.SMEM), whole, whole],
        out_specs=whole,
        name="finish",
    )(scale.reshape(1), terms, rows)


def local(image_emb, text_emb, positive, log_scale, bias):
    scale = jnp.exp(log_scale[0])
    rows, width = image_emb.shape
    mine = text_emb.shape[0]
    peers = len(TEXT_GROUPS[0])
    n_x = lax.axis_size("x")
    x = lax.axis_index("x")
    quarter = rows // n_x

    part, copies = first_copies(x.astype(jnp.int32).reshape(1), image_emb, text_emb, quarter, peers)
    parts = [swap(part, axes) for axes in ("wl", "yl", ("yl", "wl"))]
    parts = jnp.concatenate(parts, axis=0)
    texts = exchange(copies, RINGS, TEXT_GROUPS).reshape(-1, width)

    twice = jnp.concatenate([image_emb, image_emb], axis=0)
    near, far = [], []
    for d in range(n_x):
        own = lax.dynamic_slice_in_dim(twice, (x + d) * quarter, quarter, 0)
        raw = jnp.concatenate([own, parts if d == 0 else shift(parts, "x", n_x - d)], axis=0)
        near.append(unit_rows(raw)[0].astype(BF16))
        far.append(swap(near[d], "c"))
    near, far = jnp.concatenate(near, axis=0), jnp.concatenate(far, axis=0)
    text_bf = unit_rows(texts)[0].astype(BF16)

    wanted = positive - lax.axis_index(("yh", "yl", "wh", "wl", "c")) * rows
    place = lax.rem(wanted // quarter + n_x - x, n_x) * (4 * quarter) + lax.rem(wanted, quarter)
    slot = lax.axis_index(("yh", "wh")) * mine
    place = lax.dynamic_update_slice_in_dim(jnp.full((texts.shape[0],), -1, jnp.int32), place, slot, 0)
    hit = (jnp.arange(near.shape[0], dtype=jnp.int32)[:, None] == place[None, :]).astype(F32)

    def pair_grad(images):
        cosine = lax.dot_general(images, text_bf, (((1,), (1,)), ((), ())), preferred_element_type=F32)
        return jax.nn.sigmoid(scale * cosine + bias[0])

    near_grad = (pair_grad(near) - hit).astype(BF16)
    far_grad = pair_grad(far).astype(BF16)
    near_terms = jnp.dot(near_grad, text_bf, preferred_element_type=F32).reshape(n_x, -1, width)
    far_terms = jnp.dot(far_grad, text_bf, preferred_element_type=F32).astype(BF16).reshape(n_x, -1, width)
    over_images = (((0,), (0,)), ((), ()))
    text_terms = lax.dot_general(near_grad, near, over_images, preferred_element_type=F32)
    text_terms = text_terms + lax.dot_general(far_grad, far, over_images, preferred_element_type=F32)
    text_terms = exchange(text_terms.astype(BF16).reshape(peers, mine, width), RINGS, TEXT_GROUPS)

    total = None
    for d in (2, 1, 3, 0):
        terms = near_terms[d] + swap(far_terms[d], "c").astype(F32)
        terms = shift(terms.astype(BF16), "x", d).astype(F32) if d else terms
        total = terms if total is None else total + terms
    total = total.astype(BF16).reshape(2, 2, 2, rows // 8, width)
    total = jnp.where(lax.axis_index("yl") == 1, total[::-1], total)
    total = jnp.where(lax.axis_index("wl") == 1, total[:, ::-1], total)
    total, text_terms = lax.optimization_barrier((total, text_terms))
    image_terms = exchange(total.reshape(8, rows // 8, width), ("yl", "wl", "l"))

    first = lax.axis_index(NARROW) * (rows // 8)
    image_rows = lax.dynamic_slice_in_dim(image_emb, first, rows // 8, 0)
    grad_image = exchange(finish(image_terms, image_rows, scale, 8), NARROW).reshape(rows, width)
    grad_text = finish(text_terms, text_emb, scale, 1).reshape(mine, width)
    return grad_image, grad_text


def solution(mesh):
    fine = Mesh(mesh.devices.reshape(SIZES), AXES)
    dp = ("yh", "yl", "wh", "wl", "c")
    in_specs = (P(dp, None), P(AXES, None), P(AXES), P(), P())
    out_specs = (P(dp, None), P(AXES, None))
    return jax.shard_map(local, mesh=fine, in_specs=in_specs, out_specs=out_specs, check_vma=False)
```

```python
import jax
import jax.numpy as jnp
from jax import lax
from jax.experimental import pallas as pl
from jax.experimental.pallas import tpu as pltpu
from jax.sharding import Mesh, PartitionSpec as P

epsilon = 1e-06
AXES = ("yh", "yl", "w", "c", "x", "l")
CLASSES = ((0, 3, 5, 6), (1, 2, 4, 7))
RINGS = ("yh", "yl", "w", "l")
TEXT_GROUPS = [[y * 8 + z for y in of_y for z in of_z] for of_y in CLASSES for of_z in CLASSES]
NARROW = ("x", "l")
BF16, F32 = jnp.bfloat16, jnp.float32


def unit_rows(values):
    as_float = values.astype(F32)
    row_norm = jnp.sqrt(jnp.sum(as_float * as_float, axis=1, keepdims=True) + epsilon)
    return as_float / row_norm, row_norm


def swap(block, axis):
    return lax.ppermute(block, axis, [(0, 1), (1, 0)])


def shift(block, axis, distance):
    count = lax.axis_size(axis)
    return lax.ppermute(block, axis, [(i, (i + distance) % count) for i in range(count)])


def exchange(blocks, axes, groups=None):
    return lax.all_to_all(blocks, axes, 0, 0, axis_index_groups=groups, tiled=True)


def first_copies(x, image_emb, text_emb, quarter, peers):
    mine, width = text_emb.shape

    def body(x_ref, image_ref, text_ref, quarter_ref, copies_ref):
        start = pl.multiple_of(x_ref[0] * quarter, quarter)
        quarter_ref[...] = image_ref[pl.ds(start, quarter), :]
        for k in range(peers):
            copies_ref[k] = text_ref[...]

    whole = pl.BlockSpec(memory_space=pltpu.VMEM)
    return pl.pallas_call(
        body,
        out_shape=(
            jax.ShapeDtypeStruct((quarter, width), BF16),
            jax.ShapeDtypeStruct((peers, mine, width), BF16),
        ),
        in_specs=[pl.BlockSpec(memory_space=pltpu.SMEM), whole, whole],
        out_specs=(whole, whole),
        name="first_copies",
    )(x, image_emb, text_emb)


def finish(terms, unit, norm, scale):
    total = scale * jnp.sum(terms.astype(F32), axis=0)
    along = jnp.sum(unit * total, axis=1, keepdims=True)
    return ((total - unit * along) / norm).astype(BF16)


def local(image_emb, text_emb, positive, log_scale, bias):
    scale = jnp.exp(log_scale[0])
    rows, width = image_emb.shape
    mine = text_emb.shape[0]
    peers = len(TEXT_GROUPS[0])
    n_x = lax.axis_size("x")
    x = lax.axis_index("x")
    upper = lax.axis_index("yl") == 1
    quarter = rows // n_x

    part, copies = first_copies(x.astype(jnp.int32).reshape(1), image_emb, text_emb, quarter, peers)
    part = swap(part, "yl")
    texts = exchange(copies, RINGS, TEXT_GROUPS).reshape(-1, width)
    around = [part] + [shift(part, "x", n_x - d) for d in range(1, n_x)]
    beyond = lax.dynamic_slice_in_dim(jnp.concatenate(around * 2, axis=0), lax.rem(n_x - x, n_x) * quarter, rows, 0)
    chip = jnp.concatenate([jnp.where(upper, beyond, image_emb), jnp.where(upper, image_emb, beyond)], axis=0)
    near = unit_rows(chip)[0].astype(BF16)
    far = swap(near, "c")
    text_bf = unit_rows(texts)[0].astype(BF16)

    wanted = positive - lax.axis_index(("yh", "yl", "w", "c")) * rows + lax.axis_index("yl") * rows
    slot = lax.axis_index(("yh", "w")) * mine
    wanted = lax.dynamic_update_slice_in_dim(jnp.full((texts.shape[0],), -1, jnp.int32), wanted, slot, 0)
    hit = (wanted[:, None] == jnp.arange(2 * near.shape[0], dtype=jnp.int32)[None, :]).astype(F32)

    first = lax.axis_index(NARROW) * (rows // 8)
    image_unit, image_norm = unit_rows(lax.dynamic_slice_in_dim(image_emb, first, rows // 8, 0))
    text_unit, text_norm = unit_rows(text_emb)
    image_unit, image_norm, text_unit, text_norm = lax.optimization_barrier(
        (image_unit, image_norm, text_unit, text_norm)
    )

    images = jnp.concatenate([near, far], axis=0)
    cosine = lax.dot_general(text_bf, images, (((1,), (1,)), ((), ())), preferred_element_type=F32)
    grad = (jax.nn.sigmoid(scale * cosine + bias[0]) - hit).astype(BF16)
    text_terms = jnp.dot(grad, images, preferred_element_type=F32).astype(BF16)
    text_terms, grad = lax.optimization_barrier((text_terms, grad))
    text_sum = exchange(text_terms.reshape(peers, mine, width), RINGS, TEXT_GROUPS)

    def image_product(columns):
        return lax.dot_general(columns, text_bf, (((0,), (0,)), ((), ())), preferred_element_type=F32)

    half = near.shape[0]
    far_terms = swap(image_product(grad[:, half:]).astype(BF16), "c")
    both = (image_product(grad[:, :half]) + far_terms.astype(F32)).reshape(2, n_x, quarter, width)

    def of_position(k):
        return lax.dynamic_index_in_dim(both, lax.rem(x + k, n_x), axis=1, keepdims=False)

    total = of_position(0)
    for d in (2, 1, 3):
        sent = of_position(d).astype(BF16).reshape(2 * quarter, width)
        total = total + shift(sent, "x", d).astype(F32).reshape(2, quarter, width)
    total, text_sum = lax.optimization_barrier((total.astype(BF16), text_sum))
    image_sum = exchange(total.reshape(4, rows // 8, width), ("yl", "l"))
    done = finish(image_sum, image_unit, image_norm, scale)
    grad_image = exchange(jnp.broadcast_to(done[None], (8,) + done.shape), NARROW).reshape(rows, width)
    grad_text = finish(text_sum, text_unit, text_norm, scale)
    return grad_image, grad_text


def solution(mesh):
    fine = Mesh(mesh.devices.reshape(4, 2, 4, 2, 4, 2), AXES)
    dp = ("yh", "yl", "w", "c")
    in_specs = (P(dp, None), P(AXES, None), P(AXES), P(), P())
    out_specs = (P(dp, None), P(AXES, None))
    return jax.shard_map(local, mesh=fine, in_specs=in_specs, out_specs=out_specs, check_vma=False)
```

```python
import jax
import jax.numpy as jnp
from jax import lax
from jax.experimental import pallas as pl
from jax.experimental.pallas import tpu as pltpu
from jax.sharding import Mesh, PartitionSpec as P

epsilon = 1e-06
AXES = ("yh", "yl", "w", "c", "x", "l")
CLASSES = ((0, 3, 5, 6), (1, 2, 4, 7))
RINGS = ("yh", "yl", "w", "l")
TEXT_GROUPS = [[y * 8 + z for y in of_y for z in of_z] for of_y in CLASSES for of_z in CLASSES]
NARROW = ("x", "l")
BF16, F32 = jnp.bfloat16, jnp.float32


def unit_rows(values):
    as_float = values.astype(F32)
    row_norm = jnp.sqrt(jnp.sum(as_float * as_float, axis=1, keepdims=True) + epsilon)
    return as_float / row_norm, row_norm


def swap(block, axes):
    count = lax.axis_size(axes)
    return lax.ppermute(block, axes, [(i, count - 1 - i) for i in range(count)])


def shift(block, axis, distance):
    count = lax.axis_size(axis)
    return lax.ppermute(block, axis, [(i, (i + distance) % count) for i in range(count)])


def exchange(blocks, axes, groups=None):
    return lax.all_to_all(blocks, axes, 0, 0, axis_index_groups=groups, tiled=True)


def in_order(around, x):
    count, height = len(around), around[0].shape[0]
    start = lax.rem(count - x, count) * height
    return lax.dynamic_slice_in_dim(jnp.concatenate(around * 2, axis=0), start, count * height, 0)


def first_copies(x, image_emb, text_emb, quarter, peers):
    mine, width = text_emb.shape

    def body(x_ref, image_ref, text_ref, quarter_ref, copies_ref, sems):
        start = pl.multiple_of(x_ref[0] * quarter, quarter)
        copies = [pltpu.make_async_copy(image_ref.at[pl.ds(start, quarter)], quarter_ref, sems.at[peers])]
        copies += [pltpu.make_async_copy(text_ref, copies_ref.at[k], sems.at[k]) for k in range(peers)]
        for copy in copies:
            copy.start()
        for copy in copies:
            copy.wait()

    anywhere = pl.BlockSpec(memory_space=pl.ANY)
    return pl.pallas_call(
        body,
        out_shape=(
            jax.ShapeDtypeStruct((quarter, width), BF16),
            jax.ShapeDtypeStruct((peers, mine, width), BF16),
        ),
        in_specs=[pl.BlockSpec(memory_space=pltpu.SMEM), anywhere, anywhere],
        out_specs=(anywhere, anywhere),
        scratch_shapes=[pltpu.SemaphoreType.DMA((peers + 1,))],
        name="first_copies",
    )(x, image_emb, text_emb)


def finish(terms, unit, norm, scale):
    total = scale * jnp.sum(terms.astype(F32), axis=0)
    along = jnp.sum(unit * total, axis=1, keepdims=True)
    return ((total - unit * along) / norm).astype(BF16)


def local(image_emb, text_emb, positive, log_scale, bias):
    scale = jnp.exp(log_scale[0])
    rows, width = image_emb.shape
    mine = text_emb.shape[0]
    peers = len(TEXT_GROUPS[0])
    n_x = lax.axis_size("x")
    x = lax.axis_index("x")
    upper = lax.axis_index("yl") == 1
    quarter = rows // n_x

    part, copies = first_copies(x.astype(jnp.int32).reshape(1), image_emb, text_emb, quarter, peers)
    part = swap(part, "yl")
    texts = exchange(copies, RINGS, TEXT_GROUPS).reshape(-1, width)
    around = [part] + [shift(part, "x", n_x - d) for d in range(1, n_x)]
    beyond = in_order(around, x)
    chip = jnp.concatenate([jnp.where(upper, beyond, image_emb), jnp.where(upper, image_emb, beyond)], axis=0)
    near = unit_rows(chip)[0].astype(BF16)
    far = swap(near, "c")
    text_bf = unit_rows(texts)[0].astype(BF16)

    wanted = positive - lax.axis_index(("yh", "yl", "w", "c")) * rows + lax.axis_index("yl") * rows
    slot = lax.axis_index(("yh", "w")) * mine
    wanted = lax.dynamic_update_slice_in_dim(jnp.full((texts.shape[0],), -1, jnp.int32), wanted, slot, 0)
    hit = (jnp.arange(2 * near.shape[0], dtype=jnp.int32)[:, None] == wanted[None, :]).astype(F32)

    image_unit, image_norm = unit_rows(lax.dynamic_slice_in_dim(image_emb, x * quarter, quarter, 0))
    text_unit, text_norm = unit_rows(text_emb)
    image_unit, image_norm, text_unit, text_norm = lax.optimization_barrier(
        (image_unit, image_norm, text_unit, text_norm)
    )

    images = jnp.concatenate([near, far], axis=0)
    cosine = lax.dot_general(images, text_bf, (((1,), (1,)), ((), ())), preferred_element_type=F32)
    grad = (jax.nn.sigmoid(scale * cosine + bias[0]) - hit).astype(BF16)
    text_terms = lax.dot_general(grad, images, (((0,), (0,)), ((), ())), preferred_element_type=F32).astype(BF16)
    text_terms, grad = lax.optimization_barrier((text_terms, grad))
    text_sum = exchange(text_terms.reshape(peers, mine, width), RINGS, TEXT_GROUPS)

    half = near.shape[0]
    far_terms = jnp.dot(grad[half:], text_bf, preferred_element_type=F32).astype(BF16)
    far_terms = swap(far_terms, "c").astype(F32)
    both = jnp.dot(grad[:half], text_bf, preferred_element_type=F32) + far_terms
    both = both.reshape(2, n_x, quarter, width)

    def of_position(k):
        return lax.dynamic_index_in_dim(both, lax.rem(x + k, n_x), axis=1, keepdims=False)

    total = of_position(0)
    for d in (2, 1, 3):
        sent = of_position(d).astype(BF16).reshape(2 * quarter, width)
        total = total + shift(sent, "x", d).astype(F32).reshape(2, quarter, width)
    total = total.astype(BF16)
    own, other = jnp.where(upper, total[1], total[0]), jnp.where(upper, total[0], total[1])
    beside, across, corner = swap(own, "l"), swap(other, "yl"), swap(other, ("yl", "l"))
    image_sum = (own.astype(F32) + beside.astype(F32)) + (across.astype(F32) + corner.astype(F32))
    image_sum, text_sum = lax.optimization_barrier((image_sum, text_sum))
    done = finish(image_sum[None], image_unit, image_norm, scale)
    around = [done] + [shift(done, "x", n_x - d) for d in range(1, n_x)]
    grad_image = in_order(around, x)
    grad_text = finish(text_sum, text_unit, text_norm, scale)
    return grad_image, grad_text


def solution(mesh):
    fine = Mesh(mesh.devices.reshape(4, 2, 4, 2, 4, 2), AXES)
    dp = ("yh", "yl", "w", "c")
    in_specs = (P(dp, None), P(AXES, None), P(AXES), P(), P())
    out_specs = (P(dp, None), P(AXES, None))
    return jax.shard_map(local, mesh=fine, in_specs=in_specs, out_specs=out_specs, check_vma=False)
```

```python
import jax
import jax.numpy as jnp
from jax import lax
from jax.experimental import pallas as pl
from jax.experimental.pallas import tpu as pltpu
from jax.sharding import Mesh, PartitionSpec as P

epsilon = 1e-06
AXES = ("yh", "yl", "w", "c", "x", "l")
CLASSES = ((0, 3, 5, 6), (1, 2, 4, 7))
RINGS = ("yh", "yl", "w", "l")
TEXT_GROUPS = [[y * 8 + z for y in of_y for z in of_z] for of_y in CLASSES for of_z in CLASSES]
NARROW = ("x", "l")
BF16, F32 = jnp.bfloat16, jnp.float32


def unit_rows(values):
    as_float = values.astype(F32)
    row_norm = jnp.sqrt(jnp.sum(as_float * as_float, axis=1, keepdims=True) + epsilon)
    return as_float / row_norm, row_norm


def swap(block, axes):
    count = lax.axis_size(axes)
    return lax.ppermute(block, axes, [(i, count - 1 - i) for i in range(count)])


def shift(block, axis, distance):
    count = lax.axis_size(axis)
    return lax.ppermute(block, axis, [(i, (i + distance) % count) for i in range(count)])


def exchange(blocks, axes, groups=None):
    return lax.all_to_all(blocks, axes, 0, 0, axis_index_groups=groups, tiled=True)


def in_order(around, x):
    count, height = len(around), around[0].shape[0]
    start = lax.rem(count - x, count) * height
    return lax.dynamic_slice_in_dim(jnp.concatenate(around * 2, axis=0), start, count * height, 0)


def first_copies(x, image_emb, text_emb, quarter, peers):
    mine, width = text_emb.shape

    def body(x_ref, image_ref, text_ref, quarter_ref, copies_ref, sems):
        start = pl.multiple_of(x_ref[0] * quarter, quarter)
        copies = [pltpu.make_async_copy(image_ref.at[pl.ds(start, quarter)], quarter_ref, sems.at[peers])]
        copies += [pltpu.make_async_copy(text_ref, copies_ref.at[k], sems.at[k]) for k in range(peers)]
        for copy in copies:
            copy.start()
        for copy in copies:
            copy.wait()

    anywhere, whole = pl.BlockSpec(memory_space=pl.ANY), pl.BlockSpec(memory_space=pltpu.VMEM)
    return pl.pallas_call(
        body,
        out_shape=(
            jax.ShapeDtypeStruct((quarter, width), BF16),
            jax.ShapeDtypeStruct((peers, mine, width), BF16),
        ),
        in_specs=[pl.BlockSpec(memory_space=pltpu.SMEM), anywhere, whole],
        out_specs=(whole, anywhere),
        scratch_shapes=[pltpu.SemaphoreType.DMA((peers + 1,))],
        name="first_copies",
    )(x, image_emb, text_emb)


def finish(terms, unit, norm, scale):
    total = scale * jnp.sum(terms.astype(F32), axis=0)
    along = jnp.sum(unit * total, axis=1, keepdims=True)
    return ((total - unit * along) / norm).astype(BF16)


def local(image_emb, text_emb, positive, log_scale, bias):
    scale = jnp.exp(log_scale[0])
    rows, width = image_emb.shape
    mine = text_emb.shape[0]
    peers = len(TEXT_GROUPS[0])
    n_x = lax.axis_size("x")
    x = lax.axis_index("x")
    upper = lax.axis_index("yl") == 1
    quarter = rows // n_x

    part, copies = first_copies(x.astype(jnp.int32).reshape(1), image_emb, text_emb, quarter, peers)
    part = swap(part, "yl")
    texts = exchange(copies, RINGS, TEXT_GROUPS).reshape(-1, width)
    around = [part] + [shift(part, "x", n_x - d) for d in range(1, n_x)]
    beyond = in_order(around, x)
    chip = jnp.concatenate([jnp.where(upper, beyond, image_emb), jnp.where(upper, image_emb, beyond)], axis=0)
    near = unit_rows(chip)[0].astype(BF16)
    far = swap(near, "c")
    text_bf = unit_rows(texts)[0].astype(BF16)

    wanted = positive - lax.axis_index(("yh", "yl", "w", "c")) * rows + lax.axis_index("yl") * rows
    slot = lax.axis_index(("yh", "w")) * mine
    wanted = lax.dynamic_update_slice_in_dim(jnp.full((texts.shape[0],), -1, jnp.int32), wanted, slot, 0)
    hit = (jnp.arange(2 * near.shape[0], dtype=jnp.int32)[:, None] == wanted[None, :]).astype(F32)

    image_unit, image_norm = unit_rows(lax.dynamic_slice_in_dim(image_emb, x * quarter, quarter, 0))
    text_unit, text_norm = unit_rows(text_emb)
    image_unit, image_norm, text_unit, text_norm = lax.optimization_barrier(
        (image_unit, image_norm, text_unit, text_norm)
    )

    images = lax.optimization_barrier(jnp.concatenate([near, far], axis=0))
    cosine = lax.dot_general(images, text_bf, (((1,), (1,)), ((), ())), preferred_element_type=F32)
    grad = (jax.nn.sigmoid(scale * cosine + bias[0]) - hit).astype(BF16)
    text_terms = lax.dot_general(grad, images, (((0,), (0,)), ((), ())), preferred_element_type=F32).astype(BF16)
    half = near.shape[0]
    far_terms = jnp.dot(grad[half:], text_bf, preferred_element_type=F32).astype(BF16)
    far_terms = swap(far_terms, "c").astype(F32)
    both = jnp.dot(grad[:half], text_bf, preferred_element_type=F32) + far_terms
    both = both.reshape(2, n_x, quarter, width)
    text_terms, both = lax.optimization_barrier((text_terms, both))
    text_sum = exchange(text_terms.reshape(peers, mine, width), RINGS, TEXT_GROUPS)

    def of_position(k):
        return lax.dynamic_index_in_dim(both, lax.rem(x + k, n_x), axis=1, keepdims=False)

    total = of_position(0)
    for d in (2, 1, 3):
        sent = of_position(d).astype(BF16).reshape(2 * quarter, width)
        total = total + shift(sent, "x", d).astype(F32).reshape(2, quarter, width)
    total = total.astype(BF16)
    own, other = jnp.where(upper, total[1], total[0]), jnp.where(upper, total[0], total[1])
    beside, across, corner = swap(own, "l"), swap(other, "yl"), swap(other, ("yl", "l"))
    image_sum = (own.astype(F32) + beside.astype(F32)) + (across.astype(F32) + corner.astype(F32))
    done = finish(image_sum[None], image_unit, image_norm, scale)
    around = [done] + [shift(done, "x", n_x - d) for d in range(1, n_x)]
    grad_image = in_order(around, x)
    grad_text = finish(text_sum, text_unit, text_norm, scale)
    return grad_image, grad_text


def solution(mesh):
    fine = Mesh(mesh.devices.reshape(4, 2, 4, 2, 4, 2), AXES)
    dp = ("yh", "yl", "w", "c")
    in_specs = (P(dp, None), P(AXES, None), P(AXES), P(), P())
    out_specs = (P(dp, None), P(AXES, None))
    return jax.shard_map(local, mesh=fine, in_specs=in_specs, out_specs=out_specs, check_vma=False)
```

```python
import jax
import jax.numpy as jnp
from jax import lax
from jax.experimental import pallas as pl
from jax.experimental.pallas import tpu as pltpu
from jax.sharding import Mesh, PartitionSpec as P

epsilon = 1e-06
AXES = ("yh", "yl", "w", "c", "x", "l")
CLASSES = ((0, 3, 5, 6), (1, 2, 4, 7))
RINGS = ("yh", "yl", "w", "l")
TEXT_GROUPS = [[y * 8 + z for y in of_y for z in of_z] for of_y in CLASSES for of_z in CLASSES]
NARROW = ("x", "l")
BF16, F32 = jnp.bfloat16, jnp.float32


def unit_rows(values):
    as_float = values.astype(F32)
    row_norm = jnp.sqrt(jnp.sum(as_float * as_float, axis=1, keepdims=True) + epsilon)
    return as_float / row_norm, row_norm


def swap(block, axes):
    count = lax.axis_size(axes)
    return lax.ppermute(block, axes, [(i, count - 1 - i) for i in range(count)])


def shift(block, axis, distance):
    count = lax.axis_size(axis)
    return lax.ppermute(block, axis, [(i, (i + distance) % count) for i in range(count)])


def exchange(blocks, axes, groups=None):
    return lax.all_to_all(blocks, axes, 0, 0, axis_index_groups=groups, tiled=True)


def in_order(around, x):
    count, height = len(around), around[0].shape[0]
    start = lax.rem(count - x, count) * height
    return lax.dynamic_slice_in_dim(jnp.concatenate(around * 2, axis=0), start, count * height, 0)


def first_copies(x, image_emb, text_emb, quarter, peers):
    mine, width = text_emb.shape

    def body(x_ref, image_ref, text_ref, quarter_ref, copies_ref, sems):
        start = pl.multiple_of(x_ref[0] * quarter, quarter)
        copies = [pltpu.make_async_copy(image_ref.at[pl.ds(start, quarter)], quarter_ref, sems.at[peers])]
        copies += [pltpu.make_async_copy(text_ref, copies_ref.at[k], sems.at[k]) for k in range(peers)]
        for copy in copies:
            copy.start()
        for copy in copies:
            copy.wait()

    anywhere, whole = pl.BlockSpec(memory_space=pl.ANY), pl.BlockSpec(memory_space=pltpu.VMEM)
    return pl.pallas_call(
        body,
        out_shape=(
            jax.ShapeDtypeStruct((quarter, width), BF16),
            jax.ShapeDtypeStruct((peers, mine, width), BF16),
        ),
        in_specs=[pl.BlockSpec(memory_space=pltpu.SMEM), anywhere, whole],
        out_specs=(whole, anywhere),
        scratch_shapes=[pltpu.SemaphoreType.DMA((peers + 1,))],
        name="first_copies",
    )(x, image_emb, text_emb)


def finish(terms, unit, norm, scale):
    total = scale * jnp.sum(terms.astype(F32), axis=0)
    along = jnp.sum(unit * total, axis=1, keepdims=True)
    return ((total - unit * along) / norm).astype(BF16)


def local(image_emb, text_emb, positive, log_scale, bias):
    scale = jnp.exp(log_scale[0])
    rows, width = image_emb.shape
    mine = text_emb.shape[0]
    peers = len(TEXT_GROUPS[0])
    n_x = lax.axis_size("x")
    x = lax.axis_index("x")
    upper = lax.axis_index("yl") == 1
    quarter = rows // n_x

    part, copies = first_copies(x.astype(jnp.int32).reshape(1), image_emb, text_emb, quarter, peers)
    part = swap(part, "yl")
    texts = exchange(copies, RINGS, TEXT_GROUPS).reshape(-1, width)
    around = [part] + [shift(part, "x", n_x - d) for d in range(1, n_x)]
    beyond = in_order(around, x)
    chip = jnp.concatenate([jnp.where(upper, beyond, image_emb), jnp.where(upper, image_emb, beyond)], axis=0)
    near = unit_rows(chip)[0].astype(BF16)
    far = swap(near, "c")
    text_bf = unit_rows(texts)[0].astype(BF16)

    wanted = positive - lax.axis_index(("yh", "yl", "w", "c")) * rows + lax.axis_index("yl") * rows
    slot = lax.axis_index(("yh", "w")) * mine
    wanted = lax.dynamic_update_slice_in_dim(jnp.full((texts.shape[0],), -1, jnp.int32), wanted, slot, 0)
    hit = (jnp.arange(2 * near.shape[0], dtype=jnp.int32)[:, None] == wanted[None, :]).astype(F32)

    image_unit, image_norm = unit_rows(lax.dynamic_slice_in_dim(image_emb, x * quarter, quarter, 0))
    text_unit, text_norm = unit_rows(text_emb)
    image_unit, image_norm, text_unit, text_norm = lax.optimization_barrier(
        (image_unit, image_norm, text_unit, text_norm)
    )

    images = lax.optimization_barrier(jnp.concatenate([near, far], axis=0))
    cosine = lax.dot_general(images, text_bf, (((1,), (1,)), ((), ())), preferred_element_type=F32)
    grad = (jax.nn.sigmoid(scale * cosine + bias[0]) - hit).astype(BF16)
    text_terms = lax.dot_general(grad, images, (((0,), (0,)), ((), ())), preferred_element_type=F32).astype(BF16)
    text_terms, grad = lax.optimization_barrier((text_terms, grad))
    text_sum = exchange(text_terms.reshape(peers, mine, width), RINGS, TEXT_GROUPS)

    half = near.shape[0]
    far_terms = jnp.dot(grad[half:], text_bf, preferred_element_type=F32).astype(BF16)
    far_terms = swap(far_terms, "c").astype(F32)
    both = jnp.dot(grad[:half], text_bf, preferred_element_type=F32) + far_terms
    both = both.reshape(2, n_x, quarter, width)

    def of_position(k):
        return lax.dynamic_index_in_dim(both, lax.rem(x + k, n_x), axis=1, keepdims=False)

    total = of_position(0)
    for d in (2, 1, 3):
        sent = of_position(d).astype(BF16).reshape(2 * quarter, width)
        total = total + shift(sent, "x", d).astype(F32).reshape(2, quarter, width)
    total = total.astype(BF16)
    own, other = jnp.where(upper, total[1], total[0]), jnp.where(upper, total[0], total[1])
    beside, across, corner = swap(own, "l"), swap(other, "yl"), swap(other, ("yl", "l"))
    image_sum = (own.astype(F32) + beside.astype(F32)) + (across.astype(F32) + corner.astype(F32))
    image_sum, text_sum = lax.optimization_barrier((image_sum, text_sum))
    done = finish(image_sum[None], image_unit, image_norm, scale)
    grad_image = exchange(jnp.broadcast_to(done[None], (n_x,) + done.shape), "x").reshape(rows, width)
    grad_text = finish(text_sum, text_unit, text_norm, scale)
    return grad_image, grad_text


def solution(mesh):
    fine = Mesh(mesh.devices.reshape(4, 2, 4, 2, 4, 2), AXES)
    dp = ("yh", "yl", "w", "c")
    in_specs = (P(dp, None), P(AXES, None), P(AXES), P(), P())
    out_specs = (P(dp, None), P(AXES, None))
    return jax.shard_map(local, mesh=fine, in_specs=in_specs, out_specs=out_specs, check_vma=False)
```

```python
import jax
import jax.numpy as jnp
from jax import lax
from jax.experimental import pallas as pl
from jax.experimental.pallas import tpu as pltpu
from jax.sharding import Mesh, PartitionSpec as P

epsilon = 1e-06
AXES = ("yh", "yl", "w", "c", "x", "l")
CLASSES = ((0, 3, 5, 6), (1, 2, 4, 7))
RINGS = ("yh", "yl", "w", "l")
TEXT_GROUPS = [[y * 8 + z for y in of_y for z in of_z] for of_y in CLASSES for of_z in CLASSES]
NARROW = ("x", "l")
BF16, F32 = jnp.bfloat16, jnp.float32


def unit_rows(values):
    as_float = values.astype(F32)
    row_norm = jnp.sqrt(jnp.sum(as_float * as_float, axis=1, keepdims=True) + epsilon)
    return as_float / row_norm, row_norm


def swap(block, axes):
    count = lax.axis_size(axes)
    return lax.ppermute(block, axes, [(i, count - 1 - i) for i in range(count)])


def shift(block, axis, distance):
    count = lax.axis_size(axis)
    return lax.ppermute(block, axis, [(i, (i + distance) % count) for i in range(count)])


def exchange(blocks, axes, groups=None):
    return lax.all_to_all(blocks, axes, 0, 0, axis_index_groups=groups, tiled=True)


def in_order(around, x):
    count, height = len(around), around[0].shape[0]
    start = lax.rem(count - x, count) * height
    return lax.dynamic_slice_in_dim(jnp.concatenate(around * 2, axis=0), start, count * height, 0)


def first_copies(x, image_emb, text_emb, quarter, peers):
    mine, width = text_emb.shape

    def body(x_ref, image_ref, text_ref, quarter_ref, copies_ref):
        start = pl.multiple_of(x_ref[0] * quarter, quarter)
        quarter_ref[...] = image_ref[pl.ds(start, quarter), :]
        for k in range(peers):
            copies_ref[k] = text_ref[...]

    whole = pl.BlockSpec(memory_space=pltpu.VMEM)
    return pl.pallas_call(
        body,
        out_shape=(
            jax.ShapeDtypeStruct((quarter, width), BF16),
            jax.ShapeDtypeStruct((peers, mine, width), BF16),
        ),
        in_specs=[pl.BlockSpec(memory_space=pltpu.SMEM), whole, whole],
        out_specs=(whole, whole),
        name="first_copies",
    )(x, image_emb, text_emb)


def finish(terms, unit, norm, scale):
    total = scale * jnp.sum(terms.astype(F32), axis=0)
    along = jnp.sum(unit * total, axis=1, keepdims=True)
    return ((total - unit * along) / norm).astype(BF16)


def finish_late(terms, rows, scale):
    count, height, width = terms.shape

    def body(scale_ref, terms_ref, rows_ref, out_ref):
        unit, norm = unit_rows(rows_ref[...])
        out_ref[...] = finish(terms_ref[...], unit, norm, scale_ref[0])

    whole = pl.BlockSpec(memory_space=pltpu.VMEM)
    return pl.pallas_call(
        body,
        out_shape=jax.ShapeDtypeStruct((height, width), BF16),
        in_specs=[pl.BlockSpec(memory_space=pltpu.SMEM), whole, whole],
        out_specs=whole,
        cost_estimate=pl.CostEstimate(flops=40_000_000_000, bytes_accessed=100_000_000, transcendentals=0),
        name="finish_late",
    )(scale.reshape(1), terms, rows)


def local(image_emb, text_emb, positive, log_scale, bias):
    scale = jnp.exp(log_scale[0])
    rows, width = image_emb.shape
    mine = text_emb.shape[0]
    peers = len(TEXT_GROUPS[0])
    n_x = lax.axis_size("x")
    x = lax.axis_index("x")
    upper = lax.axis_index("yl") == 1
    quarter = rows // n_x

    part, copies = first_copies(x.astype(jnp.int32).reshape(1), image_emb, text_emb, quarter, peers)
    part = swap(part, "yl")
    texts = exchange(copies, RINGS, TEXT_GROUPS).reshape(-1, width)
    around = [part] + [shift(part, "x", n_x - d) for d in range(1, n_x)]
    beyond = in_order(around, x)
    chip = jnp.concatenate([jnp.where(upper, beyond, image_emb), jnp.where(upper, image_emb, beyond)], axis=0)
    near = unit_rows(chip)[0].astype(BF16)
    far = swap(near, "c")
    text_bf = unit_rows(texts)[0].astype(BF16)

    wanted = positive - lax.axis_index(("yh", "yl", "w", "c")) * rows + lax.axis_index("yl") * rows
    slot = lax.axis_index(("yh", "w")) * mine
    wanted = lax.dynamic_update_slice_in_dim(jnp.full((texts.shape[0],), -1, jnp.int32), wanted, slot, 0)
    hit = (jnp.arange(2 * near.shape[0], dtype=jnp.int32)[:, None] == wanted[None, :]).astype(F32)

    image_unit, image_norm = unit_rows(lax.dynamic_slice_in_dim(image_emb, x * quarter, quarter, 0))
    image_unit, image_norm = lax.optimization_barrier((image_unit, image_norm))

    images = lax.optimization_barrier(jnp.concatenate([near, far], axis=0))
    cosine = lax.dot_general(images, text_bf, (((1,), (1,)), ((), ())), preferred_element_type=F32)
    grad = (jax.nn.sigmoid(scale * cosine + bias[0]) - hit).astype(BF16)
    text_terms = lax.dot_general(grad, images, (((0,), (0,)), ((), ())), preferred_element_type=F32).astype(BF16)
    half = near.shape[0]
    far_terms = jnp.dot(grad[half:], text_bf, preferred_element_type=F32).astype(BF16)
    far_terms = swap(far_terms, "c").astype(F32)
    both = jnp.dot(grad[:half], text_bf, preferred_element_type=F32) + far_terms
    both = both.reshape(2, n_x, quarter, width)
    text_terms, both = lax.optimization_barrier((text_terms, both))
    text_sum = exchange(text_terms.reshape(peers, mine, width), RINGS, TEXT_GROUPS)

    def of_position(k):
        return lax.dynamic_index_in_dim(both, lax.rem(x + k, n_x), axis=1, keepdims=False)

    total = of_position(0)
    for d in (2, 1, 3):
        sent = of_position(d).astype(BF16).reshape(2 * quarter, width)
        total = total + shift(sent, "x", d).astype(F32).reshape(2, quarter, width)
    total = total.astype(BF16)
    own, other = jnp.where(upper, total[1], total[0]), jnp.where(upper, total[0], total[1])
    beside, across, corner = swap(own, "l"), swap(other, "yl"), swap(other, ("yl", "l"))
    image_sum = (own.astype(F32) + beside.astype(F32)) + (across.astype(F32) + corner.astype(F32))
    done = finish(image_sum[None], image_unit, image_norm, scale)
    around = [done] + [shift(done, "x", n_x - d) for d in range(1, n_x)]
    around, text_sum = lax.optimization_barrier((around, text_sum))
    grad_image = in_order(around, x)
    grad_text = finish_late(text_sum, text_emb, scale)
    return grad_image, grad_text


def solution(mesh):
    fine = Mesh(mesh.devices.reshape(4, 2, 4, 2, 4, 2), AXES)
    dp = ("yh", "yl", "w", "c")
    in_specs = (P(dp, None), P(AXES, None), P(AXES), P(), P())
    out_specs = (P(dp, None), P(AXES, None))
    return jax.shard_map(local, mesh=fine, in_specs=in_specs, out_specs=out_specs, check_vma=False)
```

```python
import jax
import jax.numpy as jnp
from jax import lax
from jax.experimental import pallas as pl
from jax.experimental.pallas import tpu as pltpu
from jax.sharding import Mesh, PartitionSpec as P

epsilon = 1e-06
AXES = ("yh", "yl", "w", "c", "x", "l")
CLASSES = ((0, 3, 5, 6), (1, 2, 4, 7))
RINGS = ("yh", "yl", "w", "l")
TEXT_GROUPS = [[y * 8 + z for y in of_y for z in of_z] for of_y in CLASSES for of_z in CLASSES]
NARROW = ("x", "l")
BF16, F32 = jnp.bfloat16, jnp.float32


def unit_rows(values):
    as_float = values.astype(F32)
    row_norm = jnp.sqrt(jnp.sum(as_float * as_float, axis=1, keepdims=True) + epsilon)
    return as_float / row_norm, row_norm


def swap(block, axes):
    count = lax.axis_size(axes)
    return lax.ppermute(block, axes, [(i, count - 1 - i) for i in range(count)])


def shift(block, axis, distance):
    count = lax.axis_size(axis)
    return lax.ppermute(block, axis, [(i, (i + distance) % count) for i in range(count)])


def exchange(blocks, axes, groups=None):
    return lax.all_to_all(blocks, axes, 0, 0, axis_index_groups=groups, tiled=True)


def in_order(around, x):
    count, height = len(around), around[0].shape[0]
    start = lax.rem(count - x, count) * height
    return lax.dynamic_slice_in_dim(jnp.concatenate(around * 2, axis=0), start, count * height, 0)


def first_copies(x, image_emb, text_emb, quarter, peers):
    mine, width = text_emb.shape

    def body(x_ref, image_ref, text_ref, quarter_ref, copies_ref):
        start = pl.multiple_of(x_ref[0] * quarter, quarter)
        quarter_ref[...] = image_ref[pl.ds(start, quarter), :]
        text_bf = unit_rows(text_ref[...])[0].astype(BF16)
        for k in range(peers):
            copies_ref[k] = text_bf

    whole = pl.BlockSpec(memory_space=pltpu.VMEM)
    return pl.pallas_call(
        body,
        out_shape=(
            jax.ShapeDtypeStruct((quarter, width), BF16),
            jax.ShapeDtypeStruct((peers, mine, width), BF16),
        ),
        in_specs=[pl.BlockSpec(memory_space=pltpu.SMEM), whole, whole],
        out_specs=(whole, whole),
        name="first_copies",
    )(x, image_emb, text_emb)


def finish(terms, unit, norm, scale):
    total = scale * jnp.sum(terms.astype(F32), axis=0)
    along = jnp.sum(unit * total, axis=1, keepdims=True)
    return ((total - unit * along) / norm).astype(BF16)


def local(image_emb, text_emb, positive, log_scale, bias):
    scale = jnp.exp(log_scale[0])
    rows, width = image_emb.shape
    mine = text_emb.shape[0]
    peers = len(TEXT_GROUPS[0])
    n_x = lax.axis_size("x")
    x = lax.axis_index("x")
    upper = lax.axis_index("yl") == 1
    quarter = rows // n_x

    part, copies = first_copies(x.astype(jnp.int32).reshape(1), image_emb, text_emb, quarter, peers)
    part = swap(part, "yl")
    text_bf = exchange(copies, RINGS, TEXT_GROUPS).reshape(-1, width)
    around = [part] + [shift(part, "x", n_x - d) for d in range(1, n_x)]
    beyond = in_order(around, x)
    chip = jnp.concatenate([jnp.where(upper, beyond, image_emb), jnp.where(upper, image_emb, beyond)], axis=0)
    near = unit_rows(chip)[0].astype(BF16)
    far = swap(near, "c")

    wanted = positive - lax.axis_index(("yh", "yl", "w", "c")) * rows + lax.axis_index("yl") * rows
    slot = lax.axis_index(("yh", "w")) * mine
    wanted = lax.dynamic_update_slice_in_dim(jnp.full((text_bf.shape[0],), -1, jnp.int32), wanted, slot, 0)
    hit = (jnp.arange(2 * near.shape[0], dtype=jnp.int32)[:, None] == wanted[None, :]).astype(F32)

    image_unit, image_norm = unit_rows(lax.dynamic_slice_in_dim(image_emb, x * quarter, quarter, 0))
    text_unit, text_norm = unit_rows(text_emb)
    image_unit, image_norm, text_unit, text_norm = lax.optimization_barrier(
        (image_unit, image_norm, text_unit, text_norm)
    )

    images = lax.optimization_barrier(jnp.concatenate([near, far], axis=0))
    cosine = lax.dot_general(images, text_bf, (((1,), (1,)), ((), ())), preferred_element_type=F32)
    grad = (jax.nn.sigmoid(scale * cosine + bias[0]) - hit).astype(BF16)
    text_terms = lax.dot_general(grad, images, (((0,), (0,)), ((), ())), preferred_element_type=F32).astype(BF16)
    text_terms, grad = lax.optimization_barrier((text_terms, grad))
    text_sum = exchange(text_terms.reshape(peers, mine, width), RINGS, TEXT_GROUPS)

    half = near.shape[0]
    far_terms = jnp.dot(grad[half:], text_bf, preferred_element_type=F32).astype(BF16)
    far_terms = swap(far_terms, "c").astype(F32)
    both = jnp.dot(grad[:half], text_bf, preferred_element_type=F32) + far_terms
    both = both.astype(BF16).reshape(2, n_x, quarter, width)

    def of_position(k):
        return lax.dynamic_index_in_dim(both, lax.rem(x + k, n_x), axis=1, keepdims=False)

    total = of_position(0).astype(F32)
    for d in (2, 1, 3):
        sent = of_position(d).reshape(2 * quarter, width)
        total = total + shift(sent, "x", d).astype(F32).reshape(2, quarter, width)
    total = total.astype(BF16)
    own, other = jnp.where(upper, total[1], total[0]), jnp.where(upper, total[0], total[1])
    beside, across, corner = swap(own, "l"), swap(other, "yl"), swap(other, ("yl", "l"))
    image_sum = (own.astype(F32) + beside.astype(F32)) + (across.astype(F32) + corner.astype(F32))
    image_sum, text_sum = lax.optimization_barrier((image_sum, text_sum))
    done = finish(image_sum[None], image_unit, image_norm, scale)
    grad_image = exchange(jnp.broadcast_to(done[None], (n_x,) + done.shape), "x").reshape(rows, width)
    grad_text = finish(text_sum, text_unit, text_norm, scale)
    return grad_image, grad_text


def solution(mesh):
    fine = Mesh(mesh.devices.reshape(4, 2, 4, 2, 4, 2), AXES)
    dp = ("yh", "yl", "w", "c")
    in_specs = (P(dp, None), P(AXES, None), P(AXES), P(), P())
    out_specs = (P(dp, None), P(AXES, None))
    return jax.shard_map(local, mesh=fine, in_specs=in_specs, out_specs=out_specs, check_vma=False)
```

```python
import jax
import jax.numpy as jnp
from jax import lax
from jax.experimental import pallas as pl
from jax.experimental.pallas import tpu as pltpu
from jax.sharding import Mesh, PartitionSpec as P

epsilon = 1e-06
AXES = ("yh", "yl", "w", "c", "x", "l")
CLASSES = ((0, 3, 5, 6), (1, 2, 4, 7))
RINGS = ("yh", "yl", "w", "l")
TEXT_GROUPS = [[y * 8 + z for z in of_z for y in of_y] for of_y in CLASSES for of_z in CLASSES]
NARROW = ("x", "l")
BF16, F32 = jnp.bfloat16, jnp.float32


def unit_rows(values):
    as_float = values.astype(F32)
    row_norm = jnp.sqrt(jnp.sum(as_float * as_float, axis=1, keepdims=True) + epsilon)
    return as_float / row_norm, row_norm


def swap(block, axes):
    count = lax.axis_size(axes)
    return lax.ppermute(block, axes, [(i, count - 1 - i) for i in range(count)])


def shift(block, axis, distance):
    count = lax.axis_size(axis)
    return lax.ppermute(block, axis, [(i, (i + distance) % count) for i in range(count)])


def exchange(blocks, axes, groups=None):
    return lax.all_to_all(blocks, axes, 0, 0, axis_index_groups=groups, tiled=True)


def in_order(around, x):
    count, height = len(around), around[0].shape[0]
    start = lax.rem(count - x, count) * height
    return lax.dynamic_slice_in_dim(jnp.concatenate(around * 2, axis=0), start, count * height, 0)


def first_copies(x, image_emb, text_emb, quarter, peers):
    mine, width = text_emb.shape

    def body(x_ref, image_ref, text_ref, quarter_ref, copies_ref):
        start = pl.multiple_of(x_ref[0] * quarter, quarter)
        quarter_ref[...] = image_ref[pl.ds(start, quarter), :]
        for k in range(peers):
            copies_ref[k] = text_ref[...]

    whole = pl.BlockSpec(memory_space=pltpu.VMEM)
    return pl.pallas_call(
        body,
        out_shape=(
            jax.ShapeDtypeStruct((quarter, width), BF16),
            jax.ShapeDtypeStruct((peers, mine, width), BF16),
        ),
        in_specs=[pl.BlockSpec(memory_space=pltpu.SMEM), whole, whole],
        out_specs=(whole, whole),
        name="first_copies",
    )(x, image_emb, text_emb)


def finish(terms, unit, norm, scale):
    total = scale * jnp.sum(terms.astype(F32), axis=0)
    along = jnp.sum(unit * total, axis=1, keepdims=True)
    return ((total - unit * along) / norm).astype(BF16)


def local(image_emb, text_emb, positive, log_scale, bias):
    scale = jnp.exp(log_scale[0])
    rows, width = image_emb.shape
    mine = text_emb.shape[0]
    peers = len(TEXT_GROUPS[0])
    n_x = lax.axis_size("x")
    x = lax.axis_index("x")
    upper = lax.axis_index("yl") == 1
    quarter = rows // n_x

    part, copies = first_copies(x.astype(jnp.int32).reshape(1), image_emb, text_emb, quarter, peers)
    part = swap(part, "yl")
    texts = exchange(copies, RINGS, TEXT_GROUPS).reshape(-1, width)
    around = [part] + [shift(part, "x", n_x - d) for d in range(1, n_x)]
    beyond = in_order(around, x)
    chip = jnp.concatenate([jnp.where(upper, beyond, image_emb), jnp.where(upper, image_emb, beyond)], axis=0)
    near = unit_rows(chip)[0].astype(BF16)
    far = swap(near, "c")
    text_bf = unit_rows(texts)[0].astype(BF16)

    wanted = positive - lax.axis_index(("yh", "yl", "w", "c")) * rows + lax.axis_index("yl") * rows
    slot = lax.axis_index(("w", "yh")) * mine
    wanted = lax.dynamic_update_slice_in_dim(jnp.full((texts.shape[0],), -1, jnp.int32), wanted, slot, 0)
    hit = (jnp.arange(2 * near.shape[0], dtype=jnp.int32)[:, None] == wanted[None, :]).astype(F32)

    image_unit, image_norm = unit_rows(lax.dynamic_slice_in_dim(image_emb, x * quarter, quarter, 0))
    text_unit, text_norm = unit_rows(text_emb)
    image_unit, image_norm, text_unit, text_norm = lax.optimization_barrier(
        (image_unit, image_norm, text_unit, text_norm)
    )

    images = lax.optimization_barrier(jnp.concatenate([near, far], axis=0))
    cosine = lax.dot_general(images, text_bf, (((1,), (1,)), ((), ())), preferred_element_type=F32)
    grad = (jax.nn.sigmoid(scale * cosine + bias[0]) - hit).astype(BF16)
    text_terms = lax.dot_general(grad, images, (((0,), (0,)), ((), ())), preferred_element_type=F32).astype(BF16)
    text_terms, grad = lax.optimization_barrier((text_terms, grad))
    along_z = exchange(text_terms.reshape(4, 4 * mine, width), ("w", "l"), CLASSES)

    half = near.shape[0]
    far_terms = jnp.dot(grad[half:], text_bf, preferred_element_type=F32).astype(BF16)
    far_terms = swap(far_terms, "c").astype(F32)
    both = jnp.dot(grad[:half], text_bf, preferred_element_type=F32) + far_terms
    both = both.astype(BF16).reshape(2, n_x, quarter, width)

    def of_position(k):
        return lax.dynamic_index_in_dim(both, lax.rem(x + k, n_x), axis=1, keepdims=False)

    total = of_position(0).astype(F32)
    for d in (2, 1, 3):
        sent = of_position(d).reshape(2 * quarter, width)
        total = total + shift(sent, "x", d).astype(F32).reshape(2, quarter, width)
    total = total.astype(BF16)
    own, other = jnp.where(upper, total[1], total[0]), jnp.where(upper, total[0], total[1])
    beside, across = swap(own, "l"), swap(other, "yl")
    other, along_z = lax.optimization_barrier((other, along_z))
    corner = swap(other, ("yl", "l"))
    text_sum = jnp.sum(along_z.astype(F32), axis=0).astype(BF16).reshape(4, mine, width)
    text_sum = exchange(text_sum, ("yh", "yl"), CLASSES)
    image_sum = (own.astype(F32) + beside.astype(F32)) + (across.astype(F32) + corner.astype(F32))
    done = finish(image_sum[None], image_unit, image_norm, scale)
    around = [done] + [shift(done, "x", n_x - d) for d in range(1, n_x)]
    around, text_sum = lax.optimization_barrier((around, text_sum))
    grad_image = in_order(around, x)
    grad_text = finish(text_sum, text_unit, text_norm, scale)
    return grad_image, grad_text


def solution(mesh):
    fine = Mesh(mesh.devices.reshape(4, 2, 4, 2, 4, 2), AXES)
    dp = ("yh", "yl", "w", "c")
    in_specs = (P(dp, None), P(AXES, None), P(AXES), P(), P())
    out_specs = (P(dp, None), P(AXES, None))
    return jax.shard_map(local, mesh=fine, in_specs=in_specs, out_specs=out_specs, check_vma=False)
```

```python
import jax
import jax.numpy as jnp
from jax import lax
from jax.experimental import pallas as pl
from jax.experimental.pallas import tpu as pltpu
from jax.sharding import Mesh, PartitionSpec as P

epsilon = 1e-06
AXES = ("yh", "yl", "w", "c", "x", "l")
CLASSES = ((0, 6, 3, 5), (1, 7, 2, 4))
PLACES = (0, 2, 3, 1)
RINGS = ("yh", "yl", "w", "l")
TEXT_GROUPS = [[y * 8 + z for y in of_y for z in of_z] for of_y in CLASSES for of_z in CLASSES]
NARROW = ("x", "l")
BF16, F32 = jnp.bfloat16, jnp.float32


def unit_rows(values):
    as_float = values.astype(F32)
    row_norm = jnp.sqrt(jnp.sum(as_float * as_float, axis=1, keepdims=True) + epsilon)
    return as_float / row_norm, row_norm


def swap(block, axes):
    count = lax.axis_size(axes)
    return lax.ppermute(block, axes, [(i, count - 1 - i) for i in range(count)])


def shift(block, axis, distance):
    count = lax.axis_size(axis)
    return lax.ppermute(block, axis, [(i, (i + distance) % count) for i in range(count)])


def exchange(blocks, axes, groups=None):
    return lax.all_to_all(blocks, axes, 0, 0, axis_index_groups=groups, tiled=True)


def in_order(around, x):
    count, height = len(around), around[0].shape[0]
    start = lax.rem(count - x, count) * height
    return lax.dynamic_slice_in_dim(jnp.concatenate(around * 2, axis=0), start, count * height, 0)


def first_copies(x, image_emb, text_emb, quarter, peers):
    mine, width = text_emb.shape

    def body(x_ref, image_ref, text_ref, quarter_ref, copies_ref):
        start = pl.multiple_of(x_ref[0] * quarter, quarter)
        quarter_ref[...] = image_ref[pl.ds(start, quarter), :]
        for k in range(peers):
            copies_ref[k] = text_ref[...]

    whole = pl.BlockSpec(memory_space=pltpu.VMEM)
    return pl.pallas_call(
        body,
        out_shape=(
            jax.ShapeDtypeStruct((quarter, width), BF16),
            jax.ShapeDtypeStruct((peers, mine, width), BF16),
        ),
        in_specs=[pl.BlockSpec(memory_space=pltpu.SMEM), whole, whole],
        out_specs=(whole, whole),
        name="first_copies",
    )(x, image_emb, text_emb)


def finish(terms, unit, norm, scale):
    total = scale * jnp.sum(terms.astype(F32), axis=0)
    along = jnp.sum(unit * total, axis=1, keepdims=True)
    return ((total - unit * along) / norm).astype(BF16)


def local(image_emb, text_emb, positive, log_scale, bias):
    scale = jnp.exp(log_scale[0])
    rows, width = image_emb.shape
    mine = text_emb.shape[0]
    peers = len(TEXT_GROUPS[0])
    n_x = lax.axis_size("x")
    x = lax.axis_index("x")
    upper = lax.axis_index("yl") == 1
    quarter = rows // n_x

    part, copies = first_copies(x.astype(jnp.int32).reshape(1), image_emb, text_emb, quarter, peers)
    part = swap(part, "yl")
    texts = exchange(copies, RINGS, TEXT_GROUPS).reshape(-1, width)
    around = [part] + [shift(part, "x", n_x - d) for d in range(1, n_x)]
    beyond = in_order(around, x)
    chip = jnp.concatenate([jnp.where(upper, beyond, image_emb), jnp.where(upper, image_emb, beyond)], axis=0)
    near = unit_rows(chip)[0].astype(BF16)
    far = swap(near, "c")
    text_bf = unit_rows(texts)[0].astype(BF16)

    wanted = positive - lax.axis_index(("yh", "yl", "w", "c")) * rows + lax.axis_index("yl") * rows
    places = jnp.array(PLACES, jnp.int32)
    slot = (places[lax.axis_index("yh")] * 4 + places[lax.axis_index("w")]) * mine
    wanted = lax.dynamic_update_slice_in_dim(jnp.full((texts.shape[0],), -1, jnp.int32), wanted, slot, 0)
    hit = (jnp.arange(2 * near.shape[0], dtype=jnp.int32)[:, None] == wanted[None, :]).astype(F32)

    image_unit, image_norm = unit_rows(lax.dynamic_slice_in_dim(image_emb, x * quarter, quarter, 0))
    text_unit, text_norm = unit_rows(text_emb)
    image_unit, image_norm, text_unit, text_norm = lax.optimization_barrier(
        (image_unit, image_norm, text_unit, text_norm)
    )

    images = lax.optimization_barrier(jnp.concatenate([near, far], axis=0))
    cosine = lax.dot_general(images, text_bf, (((1,), (1,)), ((), ())), preferred_element_type=F32)
    grad = (jax.nn.sigmoid(scale * cosine + bias[0]) - hit).astype(BF16)
    text_terms = lax.dot_general(grad, images, (((0,), (0,)), ((), ())), preferred_element_type=F32).astype(BF16)
    text_terms, grad = lax.optimization_barrier((text_terms, grad))
    text_sum = exchange(text_terms.reshape(peers, mine, width), RINGS, TEXT_GROUPS)

    half = near.shape[0]
    far_terms = jnp.dot(grad[half:], text_bf, preferred_element_type=F32).astype(BF16)
    far_terms = swap(far_terms, "c").astype(F32)
    both = jnp.dot(grad[:half], text_bf, preferred_element_type=F32) + far_terms
    both = both.reshape(2, n_x, quarter, width)

    def of_position(k):
        return lax.dynamic_index_in_dim(both, lax.rem(x + k, n_x), axis=1, keepdims=False)

    total = of_position(0)
    for d in (2, 1, 3):
        sent = of_position(d).astype(BF16).reshape(2 * quarter, width)
        total = total + shift(sent, "x", d).astype(F32).reshape(2, quarter, width)
    total = total.astype(BF16)
    own, other = jnp.where(upper, total[1], total[0]), jnp.where(upper, total[0], total[1])
    beside, across, corner = swap(own, "l"), swap(other, "yl"), swap(other, ("yl", "l"))
    image_sum = (own.astype(F32) + beside.astype(F32)) + (across.astype(F32) + corner.astype(F32))
    image_sum, text_sum = lax.optimization_barrier((image_sum, text_sum))
    done = finish(image_sum[None], image_unit, image_norm, scale)
    grad_image = exchange(jnp.broadcast_to(done[None], (n_x,) + done.shape), "x").reshape(rows, width)
    grad_text = finish(text_sum, text_unit, text_norm, scale)
    return grad_image, grad_text


def solution(mesh):
    fine = Mesh(mesh.devices.reshape(4, 2, 4, 2, 4, 2), AXES)
    dp = ("yh", "yl", "w", "c")
    in_specs = (P(dp, None), P(AXES, None), P(AXES), P(), P())
    out_specs = (P(dp, None), P(AXES, None))
    return jax.shard_map(local, mesh=fine, in_specs=in_specs, out_specs=out_specs, check_vma=False)
```

```python
import jax
import jax.numpy as jnp
from jax import lax
from jax.experimental import pallas as pl
from jax.experimental.pallas import tpu as pltpu
from jax.sharding import Mesh, PartitionSpec as P

epsilon = 1e-06
AXES = ("yh", "yl", "w", "c", "x", "l")
CLASSES = ((0, 3, 5, 6), (1, 2, 4, 7))
RINGS = ("yh", "yl", "w", "l")
TEXT_GROUPS = [[y * 8 + z for y in of_y for z in of_z] for of_y in CLASSES for of_z in CLASSES]
NARROW = ("x", "l")
BF16, F32 = jnp.bfloat16, jnp.float32


def unit_rows(values):
    as_float = values.astype(F32)
    row_norm = jnp.sqrt(jnp.sum(as_float * as_float, axis=1, keepdims=True) + epsilon)
    return as_float / row_norm, row_norm


def swap(block, axes):
    count = lax.axis_size(axes)
    return lax.ppermute(block, axes, [(i, count - 1 - i) for i in range(count)])


def shift(block, axis, distance):
    count = lax.axis_size(axis)
    return lax.ppermute(block, axis, [(i, (i + distance) % count) for i in range(count)])


def exchange(blocks, axes, groups=None):
    return lax.all_to_all(blocks, axes, 0, 0, axis_index_groups=groups, tiled=True)


def in_order(around, x):
    count, height = len(around), around[0].shape[0]
    start = lax.rem(count - x, count) * height
    return lax.dynamic_slice_in_dim(jnp.concatenate(around * 2, axis=0), start, count * height, 0)


def first_copies(x, image_emb, text_emb, quarter, peers):
    mine, width = text_emb.shape

    def body(x_ref, image_ref, text_ref, quarter_ref, copies_ref):
        start = pl.multiple_of(x_ref[0] * quarter, quarter)
        quarter_ref[...] = image_ref[pl.ds(start, quarter), :]
        for k in range(peers):
            copies_ref[k] = text_ref[...]

    whole = pl.BlockSpec(memory_space=pltpu.VMEM)
    return pl.pallas_call(
        body,
        out_shape=(
            jax.ShapeDtypeStruct((quarter, width), BF16),
            jax.ShapeDtypeStruct((peers, mine, width), BF16),
        ),
        in_specs=[pl.BlockSpec(memory_space=pltpu.SMEM), whole, whole],
        out_specs=(whole, whole),
        name="first_copies",
    )(x, image_emb, text_emb)


def finish(terms, unit, norm, scale):
    total = scale * jnp.sum(terms.astype(F32), axis=0)
    along = jnp.sum(unit * total, axis=1, keepdims=True)
    return ((total - unit * along) / norm).astype(BF16)


def local(image_emb, text_emb, positive, log_scale, bias):
    scale = jnp.exp(log_scale[0])
    rows, width = image_emb.shape
    mine = text_emb.shape[0]
    peers = len(TEXT_GROUPS[0])
    n_x = lax.axis_size("x")
    x = lax.axis_index("x")
    upper = lax.axis_index("yl") == 1
    quarter = rows // n_x

    part, copies = first_copies(x.astype(jnp.int32).reshape(1), image_emb, text_emb, quarter, peers)
    part = swap(part, "yl")
    texts = exchange(copies, RINGS, TEXT_GROUPS).reshape(4, 4, mine, width)
    texts = lax.optimization_barrier(texts.transpose(1, 0, 2, 3).reshape(-1, width))
    around = [part] + [shift(part, "x", n_x - d) for d in range(1, n_x)]
    beyond = in_order(around, x)
    chip = jnp.concatenate([jnp.where(upper, beyond, image_emb), jnp.where(upper, image_emb, beyond)], axis=0)
    near = unit_rows(chip)[0].astype(BF16)
    far = swap(near, "c")
    text_bf = unit_rows(texts)[0].astype(BF16)

    wanted = positive - lax.axis_index(("yh", "yl", "w", "c")) * rows + lax.axis_index("yl") * rows
    slot = lax.axis_index(("w", "yh")) * mine
    wanted = lax.dynamic_update_slice_in_dim(jnp.full((texts.shape[0],), -1, jnp.int32), wanted, slot, 0)
    hit = (jnp.arange(2 * near.shape[0], dtype=jnp.int32)[:, None] == wanted[None, :]).astype(F32)

    image_unit, image_norm = unit_rows(lax.dynamic_slice_in_dim(image_emb, x * quarter, quarter, 0))
    text_unit, text_norm = unit_rows(text_emb)
    image_unit, image_norm, text_unit, text_norm = lax.optimization_barrier(
        (image_unit, image_norm, text_unit, text_norm)
    )

    images = lax.optimization_barrier(jnp.concatenate([near, far], axis=0))
    cosine = lax.dot_general(images, text_bf, (((1,), (1,)), ((), ())), preferred_element_type=F32)
    grad = (jax.nn.sigmoid(scale * cosine + bias[0]) - hit).astype(BF16)
    text_terms = lax.dot_general(grad, images, (((0,), (0,)), ((), ())), preferred_element_type=F32).astype(BF16)
    text_terms, grad = lax.optimization_barrier((text_terms, grad))
    along_z = exchange(text_terms.reshape(4, 4 * mine, width), ("w", "l"), CLASSES)

    half = near.shape[0]
    far_terms = jnp.dot(grad[half:], text_bf, preferred_element_type=F32).astype(BF16)
    far_terms = swap(far_terms, "c").astype(F32)
    both = jnp.dot(grad[:half], text_bf, preferred_element_type=F32) + far_terms
    both = both.astype(BF16).reshape(2, n_x, quarter, width)

    def of_position(k):
        return lax.dynamic_index_in_dim(both, lax.rem(x + k, n_x), axis=1, keepdims=False)

    total = of_position(0).astype(F32)
    for d in (2, 1, 3):
        sent = of_position(d).reshape(2 * quarter, width)
        total = total + shift(sent, "x", d).astype(F32).reshape(2, quarter, width)
    total = total.astype(BF16)
    own, other = jnp.where(upper, total[1], total[0]), jnp.where(upper, total[0], total[1])
    beside, across = swap(own, "l"), swap(other, "yl")
    other, along_z = lax.optimization_barrier((other, along_z))
    corner = swap(other, ("yl", "l"))
    text_sum = jnp.sum(along_z.astype(F32), axis=0).astype(BF16).reshape(4, mine, width)
    text_sum = exchange(text_sum, ("yh", "yl"), CLASSES)
    image_sum = (own.astype(F32) + beside.astype(F32)) + (across.astype(F32) + corner.astype(F32))
    done = finish(image_sum[None], image_unit, image_norm, scale)
    around = [done] + [shift(done, "x", n_x - d) for d in range(1, n_x)]
    around, text_sum = lax.optimization_barrier((around, text_sum))
    grad_image = in_order(around, x)
    grad_text = finish(text_sum, text_unit, text_norm, scale)
    return grad_image, grad_text


def solution(mesh):
    fine = Mesh(mesh.devices.reshape(4, 2, 4, 2, 4, 2), AXES)
    dp = ("yh", "yl", "w", "c")
    in_specs = (P(dp, None), P(AXES, None), P(AXES), P(), P())
    out_specs = (P(dp, None), P(AXES, None))
    return jax.shard_map(local, mesh=fine, in_specs=in_specs, out_specs=out_specs, check_vma=False)
```

```python
import jax
import jax.numpy as jnp
from jax import lax
from jax.experimental import pallas as pl
from jax.experimental.pallas import tpu as pltpu
from jax.sharding import Mesh, PartitionSpec as P

epsilon = 1e-06
AXES = ("yh", "yl", "w", "c", "x", "l")
CLASSES = ((0, 3, 5, 6), (1, 2, 4, 7))
RINGS = ("yh", "yl", "w", "l")
TEXT_GROUPS = [[y * 8 + z for y in of_y for z in of_z] for of_y in CLASSES for of_z in CLASSES]
NARROW = ("x", "l")
BF16, F32 = jnp.bfloat16, jnp.float32


def unit_rows(values):
    as_float = values.astype(F32)
    row_norm = jnp.sqrt(jnp.sum(as_float * as_float, axis=1, keepdims=True) + epsilon)
    return as_float / row_norm, row_norm


def swap(block, axes):
    count = lax.axis_size(axes)
    return lax.ppermute(block, axes, [(i, count - 1 - i) for i in range(count)])


def shift(block, axis, distance):
    count = lax.axis_size(axis)
    return lax.ppermute(block, axis, [(i, (i + distance) % count) for i in range(count)])


def exchange(blocks, axes, groups=None):
    return lax.all_to_all(blocks, axes, 0, 0, axis_index_groups=groups, tiled=True)


def in_order(around, x):
    count, height = len(around), around[0].shape[0]
    start = lax.rem(count - x, count) * height
    return lax.dynamic_slice_in_dim(jnp.concatenate(around * 2, axis=0), start, count * height, 0)


def first_copies(x, image_emb, text_emb, quarter, peers):
    mine, width = text_emb.shape

    def body(x_ref, image_ref, text_ref, quarter_ref, copies_ref):
        start = pl.multiple_of(x_ref[0] * quarter, quarter)
        quarter_ref[...] = image_ref[pl.ds(start, quarter), :]
        for k in range(peers):
            copies_ref[k] = text_ref[...]

    whole = pl.BlockSpec(memory_space=pltpu.VMEM)
    return pl.pallas_call(
        body,
        out_shape=(
            jax.ShapeDtypeStruct((quarter, width), BF16),
            jax.ShapeDtypeStruct((peers, mine, width), BF16),
        ),
        in_specs=[pl.BlockSpec(memory_space=pltpu.SMEM), whole, whole],
        out_specs=(whole, whole),
        name="first_copies",
    )(x, image_emb, text_emb)


def finish(terms, unit, norm, scale):
    total = scale * jnp.sum(terms.astype(F32), axis=0)
    along = jnp.sum(unit * total, axis=1, keepdims=True)
    return ((total - unit * along) / norm).astype(BF16)


def local(image_emb, text_emb, positive, log_scale, bias):
    scale = jnp.exp(log_scale[0])
    rows, width = image_emb.shape
    mine = text_emb.shape[0]
    peers = len(TEXT_GROUPS[0])
    n_x = lax.axis_size("x")
    x = lax.axis_index("x")
    upper = lax.axis_index("yl") == 1
    quarter = rows // n_x

    part, copies = first_copies(x.astype(jnp.int32).reshape(1), image_emb, text_emb, quarter, peers)
    part = swap(part, "yl")
    texts = exchange(copies, RINGS, TEXT_GROUPS).reshape(4, 4, mine, width)
    texts = lax.optimization_barrier(texts.transpose(1, 0, 2, 3).reshape(-1, width))
    around = [part] + [shift(part, "x", n_x - d) for d in range(1, n_x)]
    beyond = in_order(around, x)
    chip = jnp.concatenate([jnp.where(upper, beyond, image_emb), jnp.where(upper, image_emb, beyond)], axis=0)
    near = unit_rows(chip)[0].astype(BF16)
    far = swap(near, "c")
    text_bf = unit_rows(texts)[0].astype(BF16)

    wanted = positive - lax.axis_index(("yh", "yl", "w", "c")) * rows + lax.axis_index("yl") * rows
    slot = lax.axis_index(("w", "yh")) * mine
    wanted = lax.dynamic_update_slice_in_dim(jnp.full((texts.shape[0],), -1, jnp.int32), wanted, slot, 0)
    hit = (jnp.arange(2 * near.shape[0], dtype=jnp.int32)[:, None] == wanted[None, :]).astype(F32)

    image_unit, image_norm = unit_rows(lax.dynamic_slice_in_dim(image_emb, x * quarter, quarter, 0))
    text_unit, text_norm = unit_rows(text_emb)
    image_unit, image_norm, text_unit, text_norm = lax.optimization_barrier(
        (image_unit, image_norm, text_unit, text_norm)
    )

    images = lax.optimization_barrier(jnp.concatenate([near, far], axis=0))
    cosine = lax.dot_general(images, text_bf, (((1,), (1,)), ((), ())), preferred_element_type=F32)
    grad = (jax.nn.sigmoid(scale * cosine + bias[0]) - hit).astype(BF16)
    text_terms = lax.dot_general(grad, images, (((0,), (0,)), ((), ())), preferred_element_type=F32).astype(BF16)
    text_terms, grad = lax.optimization_barrier((text_terms, grad))
    along_z = exchange(text_terms.reshape(4, 4 * mine, width), ("w", "l"), CLASSES)

    half = near.shape[0]
    far_terms = jnp.dot(grad[half:], text_bf, preferred_element_type=F32).astype(BF16)
    far_terms = swap(far_terms, "c").astype(F32)
    both = jnp.dot(grad[:half], text_bf, preferred_element_type=F32) + far_terms
    both = both.astype(BF16).reshape(2, n_x, quarter, width)

    def of_position(k):
        return lax.dynamic_index_in_dim(both, lax.rem(x + k, n_x), axis=1, keepdims=False)

    total = of_position(0).astype(F32)
    for d in (2, 1, 3):
        sent = of_position(d).reshape(2 * quarter, width)
        total = total + shift(sent, "x", d).astype(F32).reshape(2, quarter, width)
    total = total.astype(BF16)
    own, other = jnp.where(upper, total[1], total[0]), jnp.where(upper, total[0], total[1])
    beside, across = swap(own, "l"), swap(other, "yl")
    other, along_z = lax.optimization_barrier((other, along_z))
    corner = swap(other, ("yl", "l"))
    text_sum = jnp.sum(along_z.astype(F32), axis=0).astype(BF16).reshape(4, mine, width)
    text_sum = exchange(text_sum, ("yh", "yl"), CLASSES)
    image_sum = (own.astype(F32) + beside.astype(F32)) + (across.astype(F32) + corner.astype(F32))
    done = finish(image_sum[None], image_unit, image_norm, scale)
    around = {d: shift(done, "x", n_x - d) for d in (2, 1, 3)}
    around = [done] + [around[d] for d in range(1, n_x)]
    grad_text = finish(text_sum, text_unit, text_norm, scale)
    around, grad_text = lax.optimization_barrier((around, grad_text))
    grad_image = in_order(around, x)
    return grad_image, grad_text


def solution(mesh):
    fine = Mesh(mesh.devices.reshape(4, 2, 4, 2, 4, 2), AXES)
    dp = ("yh", "yl", "w", "c")
    in_specs = (P(dp, None), P(AXES, None), P(AXES), P(), P())
    out_specs = (P(dp, None), P(AXES, None))
    return jax.shard_map(local, mesh=fine, in_specs=in_specs, out_specs=out_specs, check_vma=False)
```

```python
import jax
import jax.numpy as jnp
from jax import lax
from jax.experimental import pallas as pl
from jax.experimental.pallas import tpu as pltpu
from jax.sharding import Mesh, PartitionSpec as P

epsilon = 1e-06
AXES = ("yh", "yl", "w", "c", "x", "l")
CLASSES = ((0, 3, 5, 6), (1, 2, 4, 7))
RINGS = ("yh", "yl", "w", "l")
ORDER = ((0, 0), (0, 1), (0, 2), (0, 3), (1, 2), (1, 3), (1, 0), (1, 1), (2, 0), (2, 1), (2, 2), (2, 3), (3, 2), (3, 3), (3, 0), (3, 1))
TEXT_GROUPS = [[of_y[i] * 8 + of_z[j] for i, j in ORDER] for of_y in CLASSES for of_z in CLASSES]
NARROW = ("x", "l")
BF16, F32 = jnp.bfloat16, jnp.float32


def unit_rows(values):
    as_float = values.astype(F32)
    row_norm = jnp.sqrt(jnp.sum(as_float * as_float, axis=1, keepdims=True) + epsilon)
    return as_float / row_norm, row_norm


def swap(block, axes):
    count = lax.axis_size(axes)
    return lax.ppermute(block, axes, [(i, count - 1 - i) for i in range(count)])


def shift(block, axis, distance):
    count = lax.axis_size(axis)
    return lax.ppermute(block, axis, [(i, (i + distance) % count) for i in range(count)])


def exchange(blocks, axes, groups=None):
    return lax.all_to_all(blocks, axes, 0, 0, axis_index_groups=groups, tiled=True)


def in_order(around, x):
    count, height = len(around), around[0].shape[0]
    start = lax.rem(count - x, count) * height
    return lax.dynamic_slice_in_dim(jnp.concatenate(around * 2, axis=0), start, count * height, 0)


def first_copies(x, image_emb, text_emb, quarter, peers):
    mine, width = text_emb.shape

    def body(x_ref, image_ref, text_ref, quarter_ref, copies_ref):
        start = pl.multiple_of(x_ref[0] * quarter, quarter)
        quarter_ref[...] = image_ref[pl.ds(start, quarter), :]
        for k in range(peers):
            copies_ref[k] = text_ref[...]

    whole = pl.BlockSpec(memory_space=pltpu.VMEM)
    return pl.pallas_call(
        body,
        out_shape=(
            jax.ShapeDtypeStruct((quarter, width), BF16),
            jax.ShapeDtypeStruct((peers, mine, width), BF16),
        ),
        in_specs=[pl.BlockSpec(memory_space=pltpu.SMEM), whole, whole],
        out_specs=(whole, whole),
        name="first_copies",
    )(x, image_emb, text_emb)


def finish(terms, unit, norm, scale):
    total = scale * jnp.sum(terms.astype(F32), axis=0)
    along = jnp.sum(unit * total, axis=1, keepdims=True)
    return ((total - unit * along) / norm).astype(BF16)


def local(image_emb, text_emb, positive, log_scale, bias):
    scale = jnp.exp(log_scale[0])
    rows, width = image_emb.shape
    mine = text_emb.shape[0]
    peers = len(TEXT_GROUPS[0])
    n_x = lax.axis_size("x")
    x = lax.axis_index("x")
    upper = lax.axis_index("yl") == 1
    quarter = rows // n_x

    part, copies = first_copies(x.astype(jnp.int32).reshape(1), image_emb, text_emb, quarter, peers)
    part = swap(part, "yl")
    texts = exchange(copies, RINGS, TEXT_GROUPS).reshape(peers, mine, width)
    texts = jnp.concatenate([texts[ORDER.index((i, j))] for j in range(4) for i in range(4)], axis=0)
    texts = lax.optimization_barrier(texts)
    around = [part] + [shift(part, "x", n_x - d) for d in range(1, n_x)]
    beyond = in_order(around, x)
    chip = jnp.concatenate([jnp.where(upper, beyond, image_emb), jnp.where(upper, image_emb, beyond)], axis=0)
    near = unit_rows(chip)[0].astype(BF16)
    far = swap(near, "c")
    text_bf = unit_rows(texts)[0].astype(BF16)

    wanted = positive - lax.axis_index(("yh", "yl", "w", "c")) * rows + lax.axis_index("yl") * rows
    slot = lax.axis_index(("w", "yh")) * mine
    wanted = lax.dynamic_update_slice_in_dim(jnp.full((texts.shape[0],), -1, jnp.int32), wanted, slot, 0)
    hit = (jnp.arange(2 * near.shape[0], dtype=jnp.int32)[:, None] == wanted[None, :]).astype(F32)

    image_unit, image_norm = unit_rows(lax.dynamic_slice_in_dim(image_emb, x * quarter, quarter, 0))
    text_unit, text_norm = unit_rows(text_emb)
    image_unit, image_norm, text_unit, text_norm = lax.optimization_barrier(
        (image_unit, image_norm, text_unit, text_norm)
    )

    images = lax.optimization_barrier(jnp.concatenate([near, far], axis=0))
    cosine = lax.dot_general(images, text_bf, (((1,), (1,)), ((), ())), preferred_element_type=F32)
    grad = (jax.nn.sigmoid(scale * cosine + bias[0]) - hit).astype(BF16)
    text_terms = lax.dot_general(grad, images, (((0,), (0,)), ((), ())), preferred_element_type=F32).astype(BF16)
    text_terms, grad = lax.optimization_barrier((text_terms, grad))
    along_z = exchange(text_terms.reshape(4, 4 * mine, width), ("w", "l"), CLASSES)

    half = near.shape[0]
    far_terms = jnp.dot(grad[half:], text_bf, preferred_element_type=F32).astype(BF16)
    far_terms = swap(far_terms, "c").astype(F32)
    both = jnp.dot(grad[:half], text_bf, preferred_element_type=F32) + far_terms
    both = both.astype(BF16).reshape(2, n_x, quarter, width)

    def of_position(k):
        return lax.dynamic_index_in_dim(both, lax.rem(x + k, n_x), axis=1, keepdims=False)

    total = of_position(0).astype(F32)
    for d in (2, 1, 3):
        sent = of_position(d).reshape(2 * quarter, width)
        total = total + shift(sent, "x", d).astype(F32).reshape(2, quarter, width)
    total = total.astype(BF16)
    own, other = jnp.where(upper, total[1], total[0]), jnp.where(upper, total[0], total[1])
    beside, across = swap(own, "l"), swap(other, "yl")
    other, along_z = lax.optimization_barrier((other, along_z))
    corner = swap(other, ("yl", "l"))
    text_sum = jnp.sum(along_z.astype(F32), axis=0).astype(BF16).reshape(4, mine, width)
    text_sum = exchange(text_sum, ("yh", "yl"), CLASSES)
    image_sum = (own.astype(F32) + beside.astype(F32)) + (across.astype(F32) + corner.astype(F32))
    done = finish(image_sum[None], image_unit, image_norm, scale)
    around = {d: shift(done, "x", n_x - d) for d in (2, 1, 3)}
    around = [done] + [around[d] for d in range(1, n_x)]
    grad_text = finish(text_sum, text_unit, text_norm, scale)
    around, grad_text = lax.optimization_barrier((around, grad_text))
    grad_image = in_order(around, x)
    return grad_image, grad_text


def solution(mesh):
    fine = Mesh(mesh.devices.reshape(4, 2, 4, 2, 4, 2), AXES)
    dp = ("yh", "yl", "w", "c")
    in_specs = (P(dp, None), P(AXES, None), P(AXES), P(), P())
    out_specs = (P(dp, None), P(AXES, None))
    return jax.shard_map(local, mesh=fine, in_specs=in_specs, out_specs=out_specs, check_vma=False)
```

```python
import jax
import jax.numpy as jnp
from jax import lax
from jax.experimental import pallas as pl
from jax.experimental.pallas import tpu as pltpu
from jax.sharding import Mesh, PartitionSpec as P

epsilon = 1e-06
AXES = ("yh", "yl", "w", "c", "x", "l")
CLASSES = ((0, 6, 3, 5), (1, 7, 2, 4))
PLACES = (0, 2, 3, 1)
RINGS = ("yh", "yl", "w", "l")
ORDER = ((0, 0), (0, 2), (0, 3), (0, 1), (2, 3), (2, 1), (2, 0), (2, 2), (3, 0), (3, 2), (3, 3), (3, 1), (1, 3), (1, 1), (1, 0), (1, 2))
TEXT_GROUPS = [[of_y[i] * 8 + of_z[j] for i, j in ORDER] for of_y in CLASSES for of_z in CLASSES]
NARROW = ("x", "l")
BF16, F32 = jnp.bfloat16, jnp.float32


def unit_rows(values):
    as_float = values.astype(F32)
    row_norm = jnp.sqrt(jnp.sum(as_float * as_float, axis=1, keepdims=True) + epsilon)
    return as_float / row_norm, row_norm


def swap(block, axes):
    count = lax.axis_size(axes)
    return lax.ppermute(block, axes, [(i, count - 1 - i) for i in range(count)])


def shift(block, axis, distance):
    count = lax.axis_size(axis)
    return lax.ppermute(block, axis, [(i, (i + distance) % count) for i in range(count)])


def exchange(blocks, axes, groups=None):
    return lax.all_to_all(blocks, axes, 0, 0, axis_index_groups=groups, tiled=True)


def in_order(around, x):
    count, height = len(around), around[0].shape[0]
    start = lax.rem(count - x, count) * height
    return lax.dynamic_slice_in_dim(jnp.concatenate(around * 2, axis=0), start, count * height, 0)


def first_copies(x, image_emb, text_emb, quarter, peers):
    mine, width = text_emb.shape

    def body(x_ref, image_ref, text_ref, quarter_ref, copies_ref):
        start = pl.multiple_of(x_ref[0] * quarter, quarter)
        quarter_ref[...] = image_ref[pl.ds(start, quarter), :]
        for k in range(peers):
            copies_ref[k] = text_ref[...]

    whole = pl.BlockSpec(memory_space=pltpu.VMEM)
    return pl.pallas_call(
        body,
        out_shape=(
            jax.ShapeDtypeStruct((quarter, width), BF16),
            jax.ShapeDtypeStruct((peers, mine, width), BF16),
        ),
        in_specs=[pl.BlockSpec(memory_space=pltpu.SMEM), whole, whole],
        out_specs=(whole, whole),
        name="first_copies",
    )(x, image_emb, text_emb)


def finish(terms, unit, norm, scale):
    total = scale * jnp.sum(terms.astype(F32), axis=0)
    along = jnp.sum(unit * total, axis=1, keepdims=True)
    return ((total - unit * along) / norm).astype(BF16)


def local(image_emb, text_emb, positive, log_scale, bias):
    scale = jnp.exp(log_scale[0])
    rows, width = image_emb.shape
    mine = text_emb.shape[0]
    peers = len(TEXT_GROUPS[0])
    n_x = lax.axis_size("x")
    x = lax.axis_index("x")
    upper = lax.axis_index("yl") == 1
    quarter = rows // n_x

    part, copies = first_copies(x.astype(jnp.int32).reshape(1), image_emb, text_emb, quarter, peers)
    part = swap(part, "yl")
    texts = exchange(copies, RINGS, TEXT_GROUPS).reshape(peers, mine, width)
    texts = jnp.concatenate([texts[ORDER.index((i, j))] for j in range(4) for i in range(4)], axis=0)
    texts = lax.optimization_barrier(texts)
    around = [part] + [shift(part, "x", n_x - d) for d in range(1, n_x)]
    beyond = in_order(around, x)
    chip = jnp.concatenate([jnp.where(upper, beyond, image_emb), jnp.where(upper, image_emb, beyond)], axis=0)
    near = unit_rows(chip)[0].astype(BF16)
    far = swap(near, "c")
    text_bf = unit_rows(texts)[0].astype(BF16)

    wanted = positive - lax.axis_index(("yh", "yl", "w", "c")) * rows + lax.axis_index("yl") * rows
    places = jnp.array(PLACES, jnp.int32)
    slot = (places[lax.axis_index("w")] * 4 + places[lax.axis_index("yh")]) * mine
    wanted = lax.dynamic_update_slice_in_dim(jnp.full((texts.shape[0],), -1, jnp.int32), wanted, slot, 0)
    hit = (jnp.arange(2 * near.shape[0], dtype=jnp.int32)[:, None] == wanted[None, :]).astype(F32)

    image_unit, image_norm = unit_rows(lax.dynamic_slice_in_dim(image_emb, x * quarter, quarter, 0))
    text_unit, text_norm = unit_rows(text_emb)
    image_unit, image_norm, text_unit, text_norm = lax.optimization_barrier(
        (image_unit, image_norm, text_unit, text_norm)
    )

    images = lax.optimization_barrier(jnp.concatenate([near, far], axis=0))
    cosine = lax.dot_general(images, text_bf, (((1,), (1,)), ((), ())), preferred_element_type=F32)
    grad = (jax.nn.sigmoid(scale * cosine + bias[0]) - hit).astype(BF16)
    text_terms = lax.dot_general(grad, images, (((0,), (0,)), ((), ())), preferred_element_type=F32).astype(BF16)
    text_terms, grad = lax.optimization_barrier((text_terms, grad))
    along_z = exchange(text_terms.reshape(4, 4 * mine, width), ("w", "l"), CLASSES)

    half = near.shape[0]
    far_terms = jnp.dot(grad[half:], text_bf, preferred_element_type=F32).astype(BF16)
    far_terms = swap(far_terms, "c").astype(F32)
    both = jnp.dot(grad[:half], text_bf, preferred_element_type=F32) + far_terms
    both = both.astype(BF16).reshape(2, n_x, quarter, width)

    def of_position(k):
        return lax.dynamic_index_in_dim(both, lax.rem(x + k, n_x), axis=1, keepdims=False)

    total = of_position(0).astype(F32)
    for d in (2, 1, 3):
        sent = of_position(d).reshape(2 * quarter, width)
        total = total + shift(sent, "x", d).astype(F32).reshape(2, quarter, width)
    total = total.astype(BF16)
    own, other = jnp.where(upper, total[1], total[0]), jnp.where(upper, total[0], total[1])
    beside, across = swap(own, "l"), swap(other, "yl")
    other, along_z = lax.optimization_barrier((other, along_z))
    corner = swap(other, ("yl", "l"))
    text_sum = jnp.sum(along_z.astype(F32), axis=0).astype(BF16).reshape(4, mine, width)
    text_sum = exchange(text_sum, ("yh", "yl"), CLASSES)
    image_sum = (own.astype(F32) + beside.astype(F32)) + (across.astype(F32) + corner.astype(F32))
    done = finish(image_sum[None], image_unit, image_norm, scale)
    around = {d: shift(done, "x", n_x - d) for d in (2, 1, 3)}
    around = [done] + [around[d] for d in range(1, n_x)]
    grad_text = finish(text_sum, text_unit, text_norm, scale)
    around, grad_text = lax.optimization_barrier((around, grad_text))
    grad_image = in_order(around, x)
    return grad_image, grad_text


def solution(mesh):
    fine = Mesh(mesh.devices.reshape(4, 2, 4, 2, 4, 2), AXES)
    dp = ("yh", "yl", "w", "c")
    in_specs = (P(dp, None), P(AXES, None), P(AXES), P(), P())
    out_specs = (P(dp, None), P(AXES, None))
    return jax.shard_map(local, mesh=fine, in_specs=in_specs, out_specs=out_specs, check_vma=False)
```

```python
import jax
import jax.numpy as jnp
from jax import lax
from jax.experimental import pallas as pl
from jax.experimental.pallas import tpu as pltpu
from jax.sharding import Mesh, PartitionSpec as P

epsilon = 1e-06
AXES = ("yh", "yl", "w", "c", "x", "l")
CLASSES = ((0, 5, 6, 3), (1, 4, 7, 2))
PLACES = (0, 3, 1, 2)
RINGS = ("yh", "yl", "w", "l")
ORDER = ((0, 0), (0, 3), (0, 1), (0, 2), (3, 1), (3, 2), (3, 0), (3, 3), (1, 0), (1, 3), (1, 1), (1, 2), (2, 1), (2, 2), (2, 0), (2, 3))
TEXT_GROUPS = [[of_y[i] * 8 + of_z[j] for i, j in ORDER] for of_y in CLASSES for of_z in CLASSES]
NARROW = ("x", "l")
BF16, F32 = jnp.bfloat16, jnp.float32


def unit_rows(values):
    as_float = values.astype(F32)
    row_norm = jnp.sqrt(jnp.sum(as_float * as_float, axis=1, keepdims=True) + epsilon)
    return as_float / row_norm, row_norm


def swap(block, axes):
    count = lax.axis_size(axes)
    return lax.ppermute(block, axes, [(i, count - 1 - i) for i in range(count)])


def shift(block, axis, distance):
    count = lax.axis_size(axis)
    return lax.ppermute(block, axis, [(i, (i + distance) % count) for i in range(count)])


def exchange(blocks, axes, groups=None):
    return lax.all_to_all(blocks, axes, 0, 0, axis_index_groups=groups, tiled=True)


def in_order(around, x):
    count, height = len(around), around[0].shape[0]
    start = lax.rem(count - x, count) * height
    return lax.dynamic_slice_in_dim(jnp.concatenate(around * 2, axis=0), start, count * height, 0)


def first_copies(x, image_emb, text_emb, quarter, peers):
    mine, width = text_emb.shape

    def body(x_ref, image_ref, text_ref, quarter_ref, copies_ref):
        start = pl.multiple_of(x_ref[0] * quarter, quarter)
        quarter_ref[...] = image_ref[pl.ds(start, quarter), :]
        for k in range(peers):
            copies_ref[k] = text_ref[...]

    whole = pl.BlockSpec(memory_space=pltpu.VMEM)
    return pl.pallas_call(
        body,
        out_shape=(
            jax.ShapeDtypeStruct((quarter, width), BF16),
            jax.ShapeDtypeStruct((peers, mine, width), BF16),
        ),
        in_specs=[pl.BlockSpec(memory_space=pltpu.SMEM), whole, whole],
        out_specs=(whole, whole),
        name="first_copies",
    )(x, image_emb, text_emb)


def finish(terms, unit, norm, scale):
    total = scale * jnp.sum(terms.astype(F32), axis=0)
    along = jnp.sum(unit * total, axis=1, keepdims=True)
    return ((total - unit * along) / norm).astype(BF16)


def local(image_emb, text_emb, positive, log_scale, bias):
    scale = jnp.exp(log_scale[0])
    rows, width = image_emb.shape
    mine = text_emb.shape[0]
    peers = len(TEXT_GROUPS[0])
    n_x = lax.axis_size("x")
    x = lax.axis_index("x")
    upper = lax.axis_index("yl") == 1
    quarter = rows // n_x

    part, copies = first_copies(x.astype(jnp.int32).reshape(1), image_emb, text_emb, quarter, peers)
    part = swap(part, "yl")
    texts = exchange(copies, RINGS, TEXT_GROUPS).reshape(peers, mine, width)
    texts = jnp.concatenate([texts[ORDER.index((i, j))] for j in range(4) for i in range(4)], axis=0)
    texts = lax.optimization_barrier(texts)
    around = [part] + [shift(part, "x", n_x - d) for d in range(1, n_x)]
    beyond = in_order(around, x)
    chip = jnp.concatenate([jnp.where(upper, beyond, image_emb), jnp.where(upper, image_emb, beyond)], axis=0)
    near = unit_rows(chip)[0].astype(BF16)
    far = swap(near, "c")
    text_bf = unit_rows(texts)[0].astype(BF16)

    wanted = positive - lax.axis_index(("yh", "yl", "w", "c")) * rows + lax.axis_index("yl") * rows
    places = jnp.array(PLACES, jnp.int32)
    slot = (places[lax.axis_index("w")] * 4 + places[lax.axis_index("yh")]) * mine
    wanted = lax.dynamic_update_slice_in_dim(jnp.full((texts.shape[0],), -1, jnp.int32), wanted, slot, 0)
    hit = (jnp.arange(2 * near.shape[0], dtype=jnp.int32)[:, None] == wanted[None, :]).astype(F32)

    image_unit, image_norm = unit_rows(lax.dynamic_slice_in_dim(image_emb, x * quarter, quarter, 0))
    text_unit, text_norm = unit_rows(text_emb)
    image_unit, image_norm, text_unit, text_norm = lax.optimization_barrier(
        (image_unit, image_norm, text_unit, text_norm)
    )

    images = lax.optimization_barrier(jnp.concatenate([near, far], axis=0))
    cosine = lax.dot_general(images, text_bf, (((1,), (1,)), ((), ())), preferred_element_type=F32)
    grad = (jax.nn.sigmoid(scale * cosine + bias[0]) - hit).astype(BF16)
    text_terms = lax.dot_general(grad, images, (((0,), (0,)), ((), ())), preferred_element_type=F32).astype(BF16)
    text_terms, grad = lax.optimization_barrier((text_terms, grad))
    along_z = exchange(text_terms.reshape(4, 4 * mine, width), ("w", "l"), CLASSES)

    half = near.shape[0]
    far_terms = jnp.dot(grad[half:], text_bf, preferred_element_type=F32).astype(BF16)
    far_terms = swap(far_terms, "c").astype(F32)
    both = jnp.dot(grad[:half], text_bf, preferred_element_type=F32) + far_terms
    both = both.astype(BF16).reshape(2, n_x, quarter, width)

    def of_position(k):
        return lax.dynamic_index_in_dim(both, lax.rem(x + k, n_x), axis=1, keepdims=False)

    total = of_position(0).astype(F32)
    for d in (2, 1, 3):
        sent = of_position(d).reshape(2 * quarter, width)
        total = total + shift(sent, "x", d).astype(F32).reshape(2, quarter, width)
    total = total.astype(BF16)
    own, other = jnp.where(upper, total[1], total[0]), jnp.where(upper, total[0], total[1])
    beside, across = swap(own, "l"), swap(other, "yl")
    other, along_z = lax.optimization_barrier((other, along_z))
    corner = swap(other, ("yl", "l"))
    text_sum = jnp.sum(along_z.astype(F32), axis=0).astype(BF16).reshape(4, mine, width)
    text_sum = exchange(text_sum, ("yh", "yl"), CLASSES)
    image_sum = (own.astype(F32) + beside.astype(F32)) + (across.astype(F32) + corner.astype(F32))
    done = finish(image_sum[None], image_unit, image_norm, scale)
    around = {d: shift(done, "x", n_x - d) for d in (2, 1, 3)}
    around = [done] + [around[d] for d in range(1, n_x)]
    grad_text = finish(text_sum, text_unit, text_norm, scale)
    around, grad_text = lax.optimization_barrier((around, grad_text))
    grad_image = in_order(around, x)
    return grad_image, grad_text


def solution(mesh):
    fine = Mesh(mesh.devices.reshape(4, 2, 4, 2, 4, 2), AXES)
    dp = ("yh", "yl", "w", "c")
    in_specs = (P(dp, None), P(AXES, None), P(AXES), P(), P())
    out_specs = (P(dp, None), P(AXES, None))
    return jax.shard_map(local, mesh=fine, in_specs=in_specs, out_specs=out_specs, check_vma=False)
```
